1024 devices in a mesh: seg: 64 (over x, z), curve: 16 (over y, core).
Axes of the slice: x: 8, y: 8, z: 8, core: 2. Of those that a mesh axis runs over, the one named last changes fastest.
Arguments:
- state: float32 [2048, 5, 16, 256], P(('seg', 'curve')), as said below
- new_slot: int32 [2048], P(('seg', 'curve')), may hold values from 0 to 2047, as said below
- neighbours: int32 [2048, 6], P(('seg', 'curve')), may hold values from 0 to 2047, as said below
Outputs:
- new_state: float32 [2048, 5, 16, 256], P(('seg', 'curve'))
The draws below stay inside these ranges and needn't reach their ends.
Inputs may be any that keep to these rules, and one draw needn't show every extreme that they name: `state`: densities and pressures are positive in every cell. Each box keeps its segment (32 consecutive indices, in the old and in the new order). The 2 consecutive boxes of a device go as 1 boxes to each of exactly 2 devices of its segment (possibly itself) and none to the others; new_slot is a permutation, so every device receives exactly 2 boxes. A periodic grid of boxes; each face's neighbour names the box back across the opposite face. The -z and +z neighbours of a box are owned by its own device; its -x and +x neighbours by its own device or by the device at the same curve place of the segment before (for -x) or after (for +x), cyclically; its -y and +y neighbours lie on other devices of its own segment, all 2 boxes of a device having their -y neighbours on one device and their +y neighbours on another.
All inputs are finite; a program needn't handle non-finite values.
Results may differ from the reference program's by a relative error of at most 0.00002.
Values sent between devices are 32-bit elements; how exact they have to be, the bound alone decides.
No kernel may reach another device: no remote copies, remote signals or barrier semaphores. Data moves between devices by JAX's collectives and lax.ppermute only.
A program may use at most 32 MiB of HBM per device.

```python
import math
import jax
import jax.numpy as jnp
from jax import lax

EDGE = 16
BOX_DEV = 2
BOX_SEG = 32
BOXES = 2048


def draw_state(key, part):
    key = jax.random.fold_in(key, 11)
    subkeys = jax.random.split(key, 5)
    plane_cells = EDGE * EDGE
    grid_shape = (BOXES, EDGE, plane_cells)
    box_rank = jax.random.permutation(subkeys[4], BOXES).astype(jnp.float32)
    growth = (3.0 ** (box_rank / BOXES)).reshape(BOXES, 1, 1)
    box_index = jnp.arange(BOXES, dtype=jnp.int32).reshape(BOXES, 1, 1)
    half_boxes = BOXES // 2
    density = jnp.exp(jax.random.uniform(subkeys[0], grid_shape, jnp.float32, math.log(0.5), math.log(2.0)))
    hot_box = jax.random.randint(jax.random.fold_in(subkeys[4], 2), (), half_boxes, BOXES)
    box_scale = jnp.where(box_index == hot_box, 1.3 * 3.0, growth)
    velocity = jax.random.uniform(subkeys[1], (3,) + grid_shape, jnp.float32, -0.6, 0.6) * box_scale
    pressure = jnp.exp(jax.random.uniform(subkeys[2], grid_shape, jnp.float32, math.log(0.3), math.log(1.2)))
    momentum = density[None] * velocity
    energy = pressure / 0.4 + 0.5 * density * jnp.sum(velocity * velocity, axis=0)
    return jnp.concatenate([density[:, None], jnp.moveaxis(momentum, 0, 1), energy[:, None]], axis=1).astype(jnp.float32)


def draw_new_slot(key, part):
    key = jax.random.fold_in(key, 23)
    seg_count = BOXES // BOX_SEG
    curve_count = BOX_SEG // BOX_DEV
    reach = min(BOX_DEV, curve_count)

    def one_segment(seg_index):
        seg_key = jax.random.fold_in(key, seg_index)
        subkeys = jax.random.split(seg_key, 4)
        start_order = jax.random.permutation(subkeys[0], curve_count)
        relabel = jax.random.permutation(subkeys[1], curve_count)
        offsets = jax.random.permutation(subkeys[2], curve_count)[:reach]
        slot_order = jax.random.permutation(subkeys[3], BOX_DEV)
        sources = jnp.arange(curve_count, dtype=jnp.int32)[:, None]
        box_index = jnp.arange(BOX_DEV, dtype=jnp.int32)[None, :]
        target = relabel[(start_order[sources] + offsets[box_index % reach]) % curve_count]
        return ((seg_index * curve_count + target) * BOX_DEV + slot_order[box_index]).reshape(-1)
    return jax.vmap(one_segment)(jnp.arange(seg_count, dtype=jnp.int32)).reshape(BOXES).astype(jnp.int32)


def draw_neighbours(key, part):
    key = jax.random.fold_in(key, 37)
    seg_count = BOXES // BOX_SEG
    curve_count = BOX_SEG // BOX_DEV
    depth = BOX_DEV // 2
    row_owner = jax.random.permutation(jax.random.fold_in(key, 0), curve_count).astype(jnp.int32)
    place_key = jax.random.fold_in(key, 1)

    def one_place(flat_index):
        return jax.random.permutation(jax.random.fold_in(place_key, flat_index), BOX_DEV)
    places = jax.vmap(one_place)(jnp.arange(seg_count * curve_count, dtype=jnp.int32)).astype(jnp.int32).reshape(seg_count, curve_count, BOX_DEV)
    owned = places[:, row_owner]
    seg_base = (jnp.arange(seg_count, dtype=jnp.int32) * BOX_SEG)[:, None, None]
    box_ids = seg_base + row_owner[None, :, None] * BOX_DEV + owned
    grid = box_ids.reshape(seg_count, curve_count, 2, depth).transpose(0, 2, 1, 3).reshape(2 * seg_count, curve_count, depth)
    columns = [jnp.roll(grid, 1, 0), jnp.roll(grid, -1, 0), jnp.roll(grid, 1, 1), jnp.roll(grid, -1, 1), jnp.roll(grid, 1, 2), jnp.roll(grid, -1, 2)]
    table = jnp.stack(columns, -1).reshape(-1, 6)
    return jnp.zeros((BOXES, 6), jnp.int32).at[grid.reshape(-1)].set(table).astype(jnp.int32)


def setup_inputs(seed: int = 0) -> dict:
    keys = jax.random.split(jax.random.key(seed), 4)
    return {
        "state": draw_state(jax.random.fold_in(keys[3], 71), 0),
        "new_slot": draw_new_slot(jax.random.fold_in(keys[3], 71), 0),
        "neighbours": draw_neighbours(jax.random.fold_in(keys[3], 71), 0),
    }


gamma_ratio = 1.4
courant = 0.3

def euler_flux(conserved, axis_num):
    density = conserved[0]
    moment = conserved[1:4]
    velocity = moment[axis_num] / density
    kinetic = 0.5 * (moment[0] * moment[0] + moment[1] * moment[1] + moment[2] * moment[2]) / density
    pressure = (gamma_ratio - 1.0) * (conserved[4] - kinetic)
    sound_speed = jnp.sqrt(gamma_ratio * pressure / density)
    pieces = [moment[axis_num]]
    for index in range(3):
        product_term = moment[index] * velocity
        if index == axis_num:
            product_term = product_term + pressure
        pieces.append(product_term)
    pieces.append((conserved[4] + pressure) * velocity)
    return (jnp.stack(pieces), jnp.abs(velocity) + sound_speed)

def wave_speed(cube_state):
    density = cube_state[0]
    moment = cube_state[1:4]
    kinetic = 0.5 * (moment[0] * moment[0] + moment[1] * moment[1] + moment[2] * moment[2]) / density
    pressure = (gamma_ratio - 1.0) * (cube_state[4] - kinetic)
    sound_speed = jnp.sqrt(gamma_ratio * pressure / density)
    largest = jnp.maximum(jnp.maximum(jnp.abs(moment[0]), jnp.abs(moment[1])), jnp.abs(moment[2]))
    return jnp.max(largest / density + sound_speed)

def rusanov(left, right, axis_num):
    flux_left, speed_left = euler_flux(left, axis_num)
    flux_right, speed_right = euler_flux(right, axis_num)
    fastest = jnp.maximum(speed_left, speed_right)
    return 0.5 * (flux_left + flux_right) - 0.5 * fastest[None] * (right - left)

def advance(cube_state, ghosts, step_size):
    edge = cube_state.shape[1]
    planes = ghosts.reshape(6, 5, edge, edge)
    change = jnp.zeros_like(cube_state)
    for axis_num in range(3):
        lower = jnp.expand_dims(planes[2 * axis_num], axis_num + 1)
        upper = jnp.expand_dims(planes[2 * axis_num + 1], axis_num + 1)
        extended = jnp.concatenate([lower, cube_state, upper], axis=axis_num + 1)
        left = lax.slice_in_dim(extended, 0, edge + 1, axis=axis_num + 1)
        right = lax.slice_in_dim(extended, 1, edge + 2, axis=axis_num + 1)
        fluxes = rusanov(left, right, axis_num)
        change = change + (lax.slice_in_dim(fluxes, 1, edge + 1, axis=axis_num + 1) - lax.slice_in_dim(fluxes, 0, edge, axis=axis_num + 1))
    return cube_state - step_size * change

def faces_of(cube_state):
    edge = cube_state.shape[1]
    pieces = [cube_state[:, 0], cube_state[:, -1], cube_state[:, :, 0], cube_state[:, :, -1], cube_state[:, :, :, 0], cube_state[:, :, :, -1]]
    return jnp.stack([piece.reshape(5, edge * edge) for piece in pieces])

def reference(state, new_slot, neighbours):
    edge = state.shape[2]
    moved = jnp.zeros_like(state).at[new_slot].set(state)
    cubes = moved.reshape(BOXES, 5, edge, edge, edge)
    fastest = jnp.max(lax.map(wave_speed, cubes))
    step_size = courant / fastest
    faces = lax.map(faces_of, cubes)
    opposite = jnp.array([1, 0, 3, 2, 5, 4], dtype=jnp.int32)
    ghosts = faces[neighbours, opposite[None, :]]

    def one_box(pair):
        return advance(pair[0], pair[1], step_size)
    result = lax.map(one_box, (cubes, ghosts))
    return result.reshape(state.shape)
```

```python
import jax
import jax.numpy as jnp
from jax import lax
from jax.experimental import pallas as pl
from jax.experimental.pallas import tpu as pltpu
from jax.sharding import PartitionSpec as P

gamma_ratio = 1.4
courant = 0.3

LANES = 128
ROWS = 10
SLOT = 24

vmem = pl.BlockSpec(memory_space=pltpu.VMEM)
smem = pl.BlockSpec(memory_space=pltpu.SMEM)


def lane_index(shape):
    return lax.broadcasted_iota(jnp.int32, shape, len(shape) - 1)


def primitives(cell):
    inverse = 1.0 / cell[0]
    velocity = [cell[1 + d] * inverse for d in range(3)]
    kinetic = 0.5 * (cell[1] * velocity[0] + cell[2] * velocity[1] + cell[3] * velocity[2])
    pressure = (gamma_ratio - 1.0) * (cell[4] - kinetic)
    sound = jnp.sqrt(gamma_ratio * pressure * inverse)
    return velocity, pressure, sound


def side(cell, axis_num):
    velocity, pressure, sound = primitives(cell)
    along = velocity[axis_num]
    flux = [cell[1 + axis_num]]
    for d in range(3):
        term = cell[1 + d] * along
        flux.append(term + pressure if d == axis_num else term)
    flux.append((cell[4] + pressure) * along)
    return flux, jnp.abs(along) + sound


def axis_change(cell, speed, below, above, axis_num):
    flux_below, speed_below = side(below, axis_num)
    flux_above, speed_above = side(above, axis_num)
    speed_below = jnp.maximum(speed, speed_below)
    speed_above = jnp.maximum(speed, speed_above)
    return [
        0.5 * (flux_above[v] - flux_below[v])
        - 0.5 * (speed_above * (above[v] - cell[v]) - speed_below * (cell[v] - below[v]))
        for v in range(5)
    ]


def pack_kernel(slot_ref, near_ref, state_ref, out_ref):
    count = out_ref.shape[0] // SLOT
    boxes = 2 * count
    best = None
    for box in range(2):
        cell = [state_ref[box, v] for v in range(5)]
        for v in range(5):
            for half in range(2):
                row = ROWS * box + 2 * v + half
                out_ref[pl.ds(row, count, stride=SLOT), :] = cell[v][:, LANES * half : LANES * (half + 1)]
        velocity, _, sound = primitives(cell)
        largest = jnp.maximum(jnp.maximum(jnp.abs(velocity[0]), jnp.abs(velocity[1])), jnp.abs(velocity[2]))
        speed = largest + sound
        best = speed if best is None else jnp.maximum(best, speed)
    best = jnp.max(jnp.max(best, axis=0, keepdims=True), axis=1, keepdims=True)

    def place(index):
        local = lax.rem(index, boxes)
        return lax.rem(local, 2) * count + lax.div(local, 2)

    values = [place(slot_ref[0]), place(slot_ref[1])]
    for box in range(2):
        values += [place(near_ref[box, 2]), place(near_ref[box, 3])]
    lane = lane_index((count, LANES))
    header = jnp.where(lane == 6, jnp.broadcast_to(best, lane.shape), 0.0)
    for position, value in enumerate(values):
        header = jnp.where(lane == position, value.astype(jnp.float32), header)
    out_ref[pl.ds(20, count, stride=SLOT), :] = header
    for row in range(21, SLOT):
        out_ref[pl.ds(row, count, stride=SLOT), :] = jnp.zeros((count, LANES), jnp.float32)


def exact_dot(left, right, contract):
    return lax.dot_general(
        left,
        right,
        ((contract, (0,)), ((), ())),
        precision=lax.Precision.HIGHEST,
        preferred_element_type=jnp.float32,
    )


def route_kernel(in_ref, out_ref, best_ref):
    count = in_ref.shape[0] // SLOT
    boxes = 2 * count
    header = in_ref[pl.ds(20, count, stride=SLOT), :]
    lane = lane_index((count, LANES))
    lane_f = lane.astype(jnp.float32)
    best = jnp.max(jnp.where(lane == 6, header, 0.0), axis=0, keepdims=True)
    best = jnp.max(best, axis=1, keepdims=True)
    best_ref[...] = jnp.broadcast_to(best.reshape(1, 1, 1), best_ref.shape)

    def one_hot(first, second):
        rows = [
            jnp.where(lane_f == jnp.broadcast_to(header[:, j : j + 1], lane_f.shape), 1.0, 0.0) for j in (first, second)
        ]
        return jnp.concatenate(rows, axis=0)[:, :boxes]

    columns = []
    for row in range(ROWS):
        columns.append(
            jnp.concatenate(
                [in_ref[pl.ds(ROWS * box + row, count, stride=SLOT), :] for box in range(2)], axis=0
            )
        )
    lane2 = lane_index((boxes, LANES))
    last = jnp.zeros((boxes, LANES), jnp.float32)
    first = jnp.zeros((boxes, LANES), jnp.float32)
    for v in range(5):
        mine = (lane2 >= 16 * v) & (lane2 < 16 * (v + 1))
        last = jnp.where(mine, pltpu.roll(columns[2 * v + 1], 16 * (v + 1), 1), last)
        first = jnp.where(mine, pltpu.roll(columns[2 * v], 16 * v, 1) if v else columns[0], first)
    everything = jnp.concatenate(columns + [last, first], axis=1)
    placed = exact_dot(one_hot(0, 1), everything, (0,))
    below = exact_dot(one_hot(2, 4), placed[:, ROWS * LANES : (ROWS + 1) * LANES], (1,))
    above = exact_dot(one_hot(3, 5), placed[:, (ROWS + 1) * LANES :], (1,))
    for box in range(2):
        rows = slice(count * box, count * (box + 1))
        for row in range(ROWS):
            out_ref[pl.ds(ROWS * box + row, count, stride=SLOT), :] = placed[rows, LANES * row : LANES * (row + 1)]
        out_ref[pl.ds(20 + box, count, stride=SLOT), :] = below[rows]
        out_ref[pl.ds(22 + box, count, stride=SLOT), :] = above[rows]


def load_cells(in_ref):
    count = in_ref.shape[0] // SLOT
    return [
        jnp.stack(
            [
                in_ref[pl.ds(ROWS * box + 2 * v + half, count, stride=SLOT), :]
                for box in range(2)
                for half in range(2)
            ]
        )
        for v in range(5)
    ]


def plane_kernel(near_ref, in_ref, out_ref):
    count = in_ref.shape[0] // SLOT
    cell = load_cells(in_ref)
    velocity, _, sound = primitives(cell)
    lane = lane_index(cell[0].shape)

    ghost_low = [in_ref[pl.ds(20 + box, count, stride=SLOT), :] for box in range(2)]
    ghost_high = [in_ref[pl.ds(22 + box, count, stride=SLOT), :] for box in range(2)]
    below, above = [], []
    for v in range(5):
        low = [pltpu.roll(g, LANES - 16 * v, 1) if v else g for g in ghost_low]
        high = [pltpu.roll(g, 112 - 16 * v, 1) for g in ghost_high]
        rolled = pltpu.roll(cell[v], 16, 2)
        edge = jnp.stack([low[0], rolled[0], low[1], rolled[2]])
        below.append(jnp.where(lane < 16, edge, rolled))
        rolled = pltpu.roll(cell[v], LANES - 16, 2)
        edge = jnp.stack([rolled[1], high[0], rolled[3], high[1]])
        above.append(jnp.where(lane >= LANES - 16, edge, rolled))
    change = axis_change(cell, jnp.abs(velocity[1]) + sound, below, above, 1)

    deep = lane & 15
    below, above = [], []
    slots = [[lax.rem(near_ref[box, face], 2) for box in range(2)] for face in (4, 5)]
    for v in range(5):
        wrapped = pltpu.roll(cell[v], LANES - 15, 2)
        edge = jnp.concatenate([jnp.where(slots[0][box] == 0, wrapped[0:2], wrapped[2:4]) for box in range(2)], axis=0)
        below.append(jnp.where(deep == 0, edge, pltpu.roll(cell[v], 1, 2)))
        wrapped = pltpu.roll(cell[v], 15, 2)
        edge = jnp.concatenate([jnp.where(slots[1][box] == 0, wrapped[0:2], wrapped[2:4]) for box in range(2)], axis=0)
        above.append(jnp.where(deep == 15, edge, pltpu.roll(cell[v], LANES - 1, 2)))
    more = axis_change(cell, jnp.abs(velocity[2]) + sound, below, above, 2)
    for v in range(5):
        out_ref[v] = change[v] + more[v]


def final_kernel(near_ref, in_ref, change_ref, before_ref, after_ref, best_ref, out_ref):
    count = in_ref.shape[0] // SLOT
    boxes = 2 * count
    cell = load_cells(in_ref)
    velocity, _, sound = primitives(cell)
    segment = lax.axis_index("seg")
    own_first = in_ref[0:SLOT, :]
    own_last = in_ref[SLOT * (count - 1) : SLOT * count, :]

    def ghost(face, own, other):
        chosen = []
        for box in range(2):
            index = near_ref[box, face]
            inside = lax.div(index, boxes) == segment
            rows = jnp.where(inside, own, other)
            chosen.append(jnp.where(lax.rem(index, 2) == 0, rows[0:ROWS], rows[ROWS : 2 * ROWS]))
        return chosen

    low = ghost(0, own_last, before_ref[...])
    high = ghost(1, own_first, after_ref[...])
    layer = lax.broadcasted_iota(jnp.int32, cell[0].shape, 1)
    below, above = [], []
    for v in range(5):

        def spread(rows):
            return jnp.stack([rows[box][2 * v + half : 2 * v + half + 1] for box in range(2) for half in range(2)])

        below.append(jnp.where(layer == 0, spread(low), pltpu.roll(cell[v], 1, 1)))
        above.append(jnp.where(layer == count - 1, spread(high), pltpu.roll(cell[v], count - 1, 1)))
    change = axis_change(cell, jnp.abs(velocity[0]) + sound, below, above, 0)

    best = jnp.max(best_ref[...], axis=0)
    step = courant / best
    for v in range(5):
        result = cell[v] - step[None] * (change[v] + change_ref[v])
        for box in range(2):
            for half in range(2):
                out_ref[box, v, :, LANES * half : LANES * (half + 1)] = result[2 * box + half]


def local(state, new_slot, neighbours):
    count = lax.axis_size("curve")
    segs = lax.axis_size("seg")
    f32 = jnp.float32
    rows = SLOT * count
    sent = pl.pallas_call(
        pack_kernel,
        out_shape=jax.ShapeDtypeStruct((rows, LANES), f32),
        in_specs=[smem, smem, vmem],
        out_specs=vmem,
        name="pack",
    )(new_slot, neighbours, state)
    met = lax.all_to_all(sent.reshape(count, SLOT, LANES), "curve", 0, 0, tiled=True)
    routed, best = pl.pallas_call(
        route_kernel,
        out_shape=(jax.ShapeDtypeStruct((rows, LANES), f32), jax.ShapeDtypeStruct((segs, 1, LANES), f32)),
        in_specs=[vmem],
        out_specs=(vmem, vmem),
        name="route",
    )(met.reshape(rows, LANES))
    moved = lax.all_to_all(routed.reshape(count, SLOT, LANES), "curve", 0, 0, tiled=True)
    best = lax.all_to_all(best, "seg", 0, 0, tiled=True)
    up = [(i, (i + 1) % segs) for i in range(segs)]
    down = [(j, i) for i, j in up]
    before = lax.ppermute(moved[count - 1], "seg", up)
    after = lax.ppermute(moved[0], "seg", down)
    moved = moved.reshape(rows, LANES)
    change = pl.pallas_call(
        plane_kernel,
        out_shape=jax.ShapeDtypeStruct((5, 4, count, LANES), f32),
        in_specs=[smem, vmem],
        out_specs=vmem,
        name="planes",
    )(neighbours, moved)
    return pl.pallas_call(
        final_kernel,
        out_shape=jax.ShapeDtypeStruct(state.shape, f32),
        in_specs=[smem, vmem, vmem, vmem, vmem, vmem],
        out_specs=vmem,
        name="finish",
    )(neighbours, moved, change, before, after, best)


def solution(mesh):
    placed = (P(("seg", "curve"), None, None, None), P(("seg", "curve")), P(("seg", "curve"), None))
    return jax.shard_map(
        local,
        mesh=mesh,
        in_specs=placed,
        out_specs=P(("seg", "curve"), None, None, None),
        check_vma=False,
    )
```

```python
import math

import jax
import jax.numpy as jnp
from jax import lax
from jax.experimental import pallas as pl
from jax.experimental.pallas import tpu as pltpu
from jax.sharding import Mesh, PartitionSpec as P

gamma_ratio = 1.4
courant = 0.3

LANES = 128
ROWS = 10
SLOT = 24
WIDE = 48

vmem = pl.BlockSpec(memory_space=pltpu.VMEM)
smem = pl.BlockSpec(memory_space=pltpu.SMEM)
params = pltpu.CompilerParams(vmem_limit_bytes=16 * 2**20)
SEG = ("seg_x", "seg_z")


def lane_index(shape):
    return lax.broadcasted_iota(jnp.int32, shape, len(shape) - 1)


def primitives(cell):
    inverse = 1.0 / cell[0]
    velocity = [cell[1 + d] * inverse for d in range(3)]
    kinetic = 0.5 * (cell[1] * velocity[0] + cell[2] * velocity[1] + cell[3] * velocity[2])
    pressure = (gamma_ratio - 1.0) * (cell[4] - kinetic)
    sound = jnp.sqrt(gamma_ratio * pressure * inverse)
    return velocity, pressure, sound


def side(cell, axis_num):
    velocity, pressure, sound = primitives(cell)
    along = velocity[axis_num]
    flux = [cell[1 + axis_num]]
    for d in range(3):
        term = cell[1 + d] * along
        flux.append(term + pressure if d == axis_num else term)
    flux.append((cell[4] + pressure) * along)
    return flux, jnp.abs(along) + sound


def axis_change(cell, speed, below, above, axis_num):
    flux_below, speed_below = side(below, axis_num)
    flux_above, speed_above = side(above, axis_num)
    speed_below = jnp.maximum(speed, speed_below)
    speed_above = jnp.maximum(speed, speed_above)
    return [
        0.5 * (flux_above[v] - flux_below[v])
        - 0.5 * (speed_above * (above[v] - cell[v]) - speed_below * (cell[v] - below[v]))
        for v in range(5)
    ]


def pack_kernel(slot_ref, near_ref, state_ref, out_ref, pick_ref):
    count = out_ref.shape[0] // SLOT
    boxes = 2 * count
    best = None
    for box in range(2):
        cell = [state_ref[box, v] for v in range(5)]
        for v in range(5):
            for half in range(2):
                row = ROWS * box + 2 * v + half
                out_ref[pl.ds(row, count, stride=SLOT), :] = cell[v][:, LANES * half : LANES * (half + 1)]
        velocity, _, sound = primitives(cell)
        largest = jnp.maximum(jnp.maximum(jnp.abs(velocity[0]), jnp.abs(velocity[1])), jnp.abs(velocity[2]))
        speed = largest + sound
        best = speed if best is None else jnp.maximum(best, speed)
    best = jnp.max(jnp.max(best, axis=0, keepdims=True), axis=1, keepdims=True)

    def place(index):
        local = lax.rem(index, boxes)
        return lax.rem(local, 2) * count + lax.div(local, 2)

    values = [place(slot_ref[0]), place(slot_ref[1])]
    for box in range(2):
        values += [place(near_ref[box, 2]), place(near_ref[box, 3])]
    lane = lane_index((count, LANES))
    header = jnp.where(lane == 6, jnp.broadcast_to(best, lane.shape), 0.0)
    for position, value in enumerate(values):
        header = jnp.where(lane == position, value.astype(jnp.float32), header)
    out_ref[pl.ds(20, count, stride=SLOT), :] = header
    for row in range(21, SLOT):
        out_ref[pl.ds(row, count, stride=SLOT), :] = jnp.zeros((count, LANES), jnp.float32)

    segment = lax.axis_index(SEG)
    lane = lane_index(pick_ref.shape)
    picks = jnp.zeros(pick_ref.shape, jnp.float32)
    for box in range(2):
        for face in (0, 1, 4, 5):
            index = near_ref[box, face]
            value = lax.rem(index, 2)
            if face < 2:
                value = value + jnp.where(lax.div(index, boxes) == segment, 2, 0)
            picks = jnp.where(lane == 6 * box + face, value.astype(jnp.float32), picks)
    pick_ref[...] = picks


def peak_kernel(in_ref, best_ref):
    count = in_ref.shape[0] // SLOT
    header = in_ref[pl.ds(20, count, stride=SLOT), :]
    best = jnp.max(jnp.where(lane_index(header.shape) == 6, header, 0.0), axis=0, keepdims=True)
    best = jnp.max(best, axis=1, keepdims=True)
    best_ref[...] = jnp.broadcast_to(best.reshape(1, 1, 1), best_ref.shape)


def three_parts(value):
    high = value.astype(jnp.bfloat16)
    rest = value - high.astype(jnp.float32)
    middle = rest.astype(jnp.bfloat16)
    low = (rest - middle.astype(jnp.float32)).astype(jnp.bfloat16)
    return jnp.concatenate([high, middle, low], axis=0)


def gather_rows(one_hot, parts):
    chosen = jnp.where(one_hot, 1.0, 0.0).astype(jnp.bfloat16)
    return jnp.dot(jnp.concatenate([chosen] * 3, axis=1), parts, preferred_element_type=jnp.float32)


def route_kernel(in_ref, before_ref, after_ref, out_ref):
    count = in_ref.shape[0] // SLOT
    boxes = 2 * count
    header = in_ref[pl.ds(20, count, stride=SLOT), :]
    lane = lane_index((count, LANES))
    both = jnp.concatenate([header, pltpu.roll(header, LANES - 1, 1)], axis=0)
    target = jnp.broadcast_to(jnp.transpose(both)[0:1, :], (boxes, boxes))
    index = lax.broadcasted_iota(jnp.int32, (boxes, boxes), 0).astype(jnp.float32)

    def beside(first, second):
        rows = jnp.concatenate([header[:, first : first + 1], header[:, second : second + 1]], axis=0)
        return jnp.broadcast_to(rows, (boxes, boxes))

    columns = []
    for row in range(ROWS):
        columns.append(
            jnp.concatenate(
                [in_ref[pl.ds(ROWS * box + row, count, stride=SLOT), :] for box in range(2)], axis=0
            )
        )
    lane2 = lane_index((boxes, LANES))
    last = jnp.zeros((boxes, LANES), jnp.float32)
    first = jnp.zeros((boxes, LANES), jnp.float32)
    for v in range(5):
        mine = (lane2 >= 16 * v) & (lane2 < 16 * (v + 1))
        last = jnp.where(mine, pltpu.roll(columns[2 * v + 1], 16 * (v + 1), 1), last)
        first = jnp.where(mine, pltpu.roll(columns[2 * v], 16 * v, 1) if v else columns[0], first)
    placed = gather_rows(index == target, three_parts(jnp.concatenate(columns, axis=1)))
    below = gather_rows(beside(2, 4) == target, three_parts(last))
    above = gather_rows(beside(3, 5) == target, three_parts(first))
    for box in range(2):
        rows = slice(count * box, count * (box + 1))
        for row in range(ROWS):
            out_ref[pl.ds(ROWS * box + row, count, stride=WIDE), :] = placed[rows, LANES * row : LANES * (row + 1)]
        out_ref[pl.ds(20 + box, count, stride=WIDE), :] = below[rows]
        out_ref[pl.ds(22 + box, count, stride=WIDE), :] = above[rows]

    place = lax.broadcasted_iota(jnp.int32, (count, LANES), 0).astype(jnp.float32)
    marks = jnp.zeros((count, LANES), jnp.float32)
    for side_num, face_ref in enumerate((after_ref, before_ref)):
        face = face_ref[...]
        target = [jnp.broadcast_to(face[20:21, box : box + 1], place.shape) for box in range(2)]
        slot = [jnp.where(t >= count, 1.0, 0.0) for t in target]
        here = [place == target[box] - count * slot[box] for box in range(2)]
        for row in range(ROWS):
            value = jnp.where(here[0], face[row : row + 1], face[ROWS + row : ROWS + row + 1])
            out_ref[pl.ds(24 + ROWS * side_num + row, count, stride=WIDE), :] = value
        mark = jnp.where(here[0], slot[0], jnp.where(here[1], slot[1], -1.0))
        marks = jnp.where(lane == side_num, mark, marks)
    for row in range(44, WIDE):
        out_ref[pl.ds(row, count, stride=WIDE), :] = marks


def advance_kernel(pick_ref, in_ref, best_ref, out_ref):
    count = in_ref.shape[0] // WIDE

    def rows_of(row):
        return in_ref[pl.ds(row, count, stride=WIDE), :]

    def pick(box, face):
        return pick_ref[0:1, 6 * box + face : 6 * box + face + 1]

    cell = [
        jnp.stack([rows_of(ROWS * box + 2 * v + half) for box in range(2) for half in range(2)]) for v in range(5)
    ]
    velocity, _, sound = primitives(cell)
    lane = lane_index(cell[0].shape)

    marks = rows_of(44)
    own = (in_ref[WIDE * (count - 1) : WIDE * (count - 1) + SLOT, :], in_ref[0:SLOT, :])
    ghosts = []
    for face in range(2):
        start = 34 - ROWS * face
        mark = jnp.broadcast_to(marks[:, 1 - face : 2 - face], (count, LANES))
        strips = [rows_of(start + row) for row in range(ROWS)]
        for box in range(2):
            wanted = pick(box, face)
            mine = mark == wanted
            far = [jnp.sum(jnp.where(mine, strip, 0.0), axis=0, keepdims=True) for strip in strips]
            near = jnp.where(wanted == 2.0, own[face][0:ROWS], own[face][ROWS : 2 * ROWS])
            inside = wanted >= 2.0
            ghosts.append([jnp.where(inside, near[row : row + 1], far[row]) for row in range(ROWS)])
    layer = lax.broadcasted_iota(jnp.int32, cell[0].shape, 1)
    below, above = [], []
    for v in range(5):

        def spread(rows):
            return jnp.stack([rows[box][2 * v + half] for box in range(2) for half in range(2)])

        below.append(jnp.where(layer == 0, spread(ghosts[0:2]), pltpu.roll(cell[v], 1, 1)))
        above.append(jnp.where(layer == count - 1, spread(ghosts[2:4]), pltpu.roll(cell[v], count - 1, 1)))
    change = axis_change(cell, jnp.abs(velocity[0]) + sound, below, above, 0)

    ghost_low = [rows_of(20 + box) for box in range(2)]
    ghost_high = [rows_of(22 + box) for box in range(2)]
    below, above = [], []
    for v in range(5):
        low = [pltpu.roll(g, LANES - 16 * v, 1) if v else g for g in ghost_low]
        high = [pltpu.roll(g, 112 - 16 * v, 1) for g in ghost_high]
        rolled = pltpu.roll(cell[v], 16, 2)
        edge = jnp.stack([low[0], rolled[0], low[1], rolled[2]])
        below.append(jnp.where(lane < 16, edge, rolled))
        rolled = pltpu.roll(cell[v], LANES - 16, 2)
        edge = jnp.stack([rolled[1], high[0], rolled[3], high[1]])
        above.append(jnp.where(lane >= LANES - 16, edge, rolled))
    more = axis_change(cell, jnp.abs(velocity[1]) + sound, below, above, 1)
    change = [change[v] + more[v] for v in range(5)]

    deep = lane & 15
    below, above = [], []
    slots = [[pick(box, face) == 0.0 for box in range(2)] for face in (4, 5)]
    for v in range(5):
        wrapped = pltpu.roll(cell[v], LANES - 15, 2)
        edge = jnp.concatenate([jnp.where(slots[0][box], wrapped[0:2], wrapped[2:4]) for box in range(2)], axis=0)
        below.append(jnp.where(deep == 0, edge, pltpu.roll(cell[v], 1, 2)))
        wrapped = pltpu.roll(cell[v], 15, 2)
        edge = jnp.concatenate([jnp.where(slots[1][box], wrapped[0:2], wrapped[2:4]) for box in range(2)], axis=0)
        above.append(jnp.where(deep == 15, edge, pltpu.roll(cell[v], LANES - 1, 2)))
    more = axis_change(cell, jnp.abs(velocity[2]) + sound, below, above, 2)

    step = courant / jnp.max(best_ref[...], axis=0)
    for v in range(5):
        result = cell[v] - step[None] * (change[v] + more[v])
        for box in range(2):
            for half in range(2):
                out_ref[box, v, :, LANES * half : LANES * (half + 1)] = result[2 * box + half]


def local(state, new_slot, neighbours):
    count = lax.axis_size("curve")
    along_x, along_z = (lax.axis_size(axis) for axis in SEG)
    segs = along_x * along_z
    f32 = jnp.float32
    sent, pick = pl.pallas_call(
        pack_kernel,
        out_shape=(jax.ShapeDtypeStruct((SLOT * count, LANES), f32), jax.ShapeDtypeStruct((8, LANES), f32)),
        in_specs=[smem, smem, vmem],
        out_specs=(vmem, vmem),
        compiler_params=params,
        name="pack",
    )(new_slot, neighbours, state)
    up = [(i, (i + 1) % segs) for i in range(segs)]
    down = [(j, i) for i, j in up]
    met = lax.all_to_all(sent.reshape(count, SLOT, LANES), "curve", 0, 0, tiled=True)
    before = lax.ppermute(sent[SLOT * (count - 1) :], SEG, up)
    after = lax.ppermute(sent[:SLOT], SEG, down)
    met = met.reshape(SLOT * count, LANES)
    best = pl.pallas_call(
        peak_kernel,
        out_shape=jax.ShapeDtypeStruct((along_x, 1, LANES), f32),
        in_specs=[vmem],
        out_specs=vmem,
        compiler_params=params,
        name="peak",
    )(met)
    best = lax.all_to_all(best, SEG[0], 0, 0, tiled=True)
    routed = pl.pallas_call(
        route_kernel,
        out_shape=jax.ShapeDtypeStruct((WIDE * count, LANES), f32),
        in_specs=[vmem, vmem, vmem],
        out_specs=vmem,
        compiler_params=params,
        name="route",
    )(met, before, after)
    moved = lax.all_to_all(routed.reshape(count, WIDE, LANES), "curve", 0, 0, tiled=True)
    best = lax.all_gather(best, SEG[1], axis=0, tiled=True)
    return pl.pallas_call(
        advance_kernel,
        out_shape=jax.ShapeDtypeStruct(state.shape, f32),
        in_specs=[vmem, vmem, vmem],
        out_specs=vmem,
        compiler_params=params,
        name="advance",
    )(pick, moved.reshape(WIDE * count, LANES), best)


def solution(mesh):
    segs, count = mesh.devices.shape
    side_x = math.isqrt(segs)
    grid = Mesh(mesh.devices.reshape(side_x, segs // side_x, count), SEG + ("curve",))
    placed = P(SEG + ("curve",))
    return jax.shard_map(
        local, mesh=grid, in_specs=(placed, placed, placed), out_specs=placed, check_vma=False
    )
```

```python
import jax
import jax.numpy as jnp
from jax import lax
from jax.experimental import pallas as pl
from jax.experimental.pallas import tpu as pltpu
from jax.sharding import PartitionSpec as P

gamma_ratio = 1.4
courant = 0.3

LANES = 128
ROWS = 10
SLOT = 24

vmem = pl.BlockSpec(memory_space=pltpu.VMEM)
hbm = pl.BlockSpec(memory_space=pltpu.HBM)
params = pltpu.CompilerParams(vmem_limit_bytes=16 * 2**20)


def lane_index(shape):
    return lax.broadcasted_iota(jnp.int32, shape, len(shape) - 1)


def primitives(cell):
    inverse = 1.0 / cell[0]
    velocity = [cell[1 + d] * inverse for d in range(3)]
    kinetic = 0.5 * (cell[1] * velocity[0] + cell[2] * velocity[1] + cell[3] * velocity[2])
    pressure = (gamma_ratio - 1.0) * (cell[4] - kinetic)
    sound = jnp.sqrt(gamma_ratio * pressure * inverse)
    return velocity, pressure, sound


def side(cell, axis_num):
    velocity, pressure, sound = primitives(cell)
    along = velocity[axis_num]
    flux = [cell[1 + axis_num]]
    for d in range(3):
        term = cell[1 + d] * along
        flux.append(term + pressure if d == axis_num else term)
    flux.append((cell[4] + pressure) * along)
    return flux, jnp.abs(along) + sound


def axis_change(cell, speed, below, above, axis_num):
    flux_below, speed_below = side(below, axis_num)
    flux_above, speed_above = side(above, axis_num)
    speed_below = jnp.maximum(speed, speed_below)
    speed_above = jnp.maximum(speed, speed_above)
    return [
        0.5 * (flux_above[v] - flux_below[v])
        - 0.5 * (speed_above * (above[v] - cell[v]) - speed_below * (cell[v] - below[v]))
        for v in range(5)
    ]


def pack_kernel(slot_hbm, near_hbm, state_hbm, out_ref, pick_ref, slot_ref, near_ref, state_ref, sems):
    copies = [
        pltpu.make_async_copy(source, target, sems.at[i])
        for i, (source, target) in enumerate(
            ((state_hbm, state_ref), (slot_hbm, slot_ref), (near_hbm, near_ref))
        )
    ]
    for copy in copies:
        copy.start()
    for copy in copies:
        copy.wait()
    count = out_ref.shape[0] // SLOT
    boxes = 2 * count
    best = None
    for box in range(2):
        cell = [state_ref[box, v] for v in range(5)]
        for v in range(5):
            for half in range(2):
                row = ROWS * box + 2 * v + half
                out_ref[pl.ds(row, count, stride=SLOT), :] = cell[v][:, LANES * half : LANES * (half + 1)]
        velocity, _, sound = primitives(cell)
        largest = jnp.maximum(jnp.maximum(jnp.abs(velocity[0]), jnp.abs(velocity[1])), jnp.abs(velocity[2]))
        speed = largest + sound
        best = speed if best is None else jnp.maximum(best, speed)
    best = jnp.max(jnp.max(best, axis=0, keepdims=True), axis=1, keepdims=True)

    def place(index):
        local = lax.rem(index, boxes)
        return lax.rem(local, 2) * count + lax.div(local, 2)

    values = [place(slot_ref[0]), place(slot_ref[1])]
    for box in range(2):
        values += [place(near_ref[box, 2]), place(near_ref[box, 3])]
    lane = lane_index((count, LANES))
    header = jnp.where(lane == 6, jnp.broadcast_to(best, lane.shape), 0.0)
    for position, value in enumerate(values):
        header = jnp.where(lane == position, value.astype(jnp.float32), header)
    out_ref[pl.ds(20, count, stride=SLOT), :] = header
    for row in range(21, SLOT):
        out_ref[pl.ds(row, count, stride=SLOT), :] = jnp.zeros((count, LANES), jnp.float32)

    segment = lax.axis_index("seg")
    lane = lane_index(pick_ref.shape)
    picks = jnp.zeros(pick_ref.shape, jnp.float32)
    for box in range(2):
        for face in (0, 1, 4, 5):
            index = near_ref[box, face]
            value = lax.rem(index, 2)
            if face < 2:
                value = value + jnp.where(lax.div(index, boxes) == segment, 2, 0)
            picks = jnp.where(lane == 6 * box + face, value.astype(jnp.float32), picks)
    pick_ref[...] = picks


def three_parts(value):
    high = value.astype(jnp.bfloat16)
    rest = value - high.astype(jnp.float32)
    middle = rest.astype(jnp.bfloat16)
    low = (rest - middle.astype(jnp.float32)).astype(jnp.bfloat16)
    return jnp.concatenate([high, middle, low], axis=0)


def gather_rows(one_hot, parts):
    chosen = jnp.where(one_hot, 1.0, 0.0).astype(jnp.bfloat16)
    return jnp.dot(jnp.concatenate([chosen] * 3, axis=1), parts, preferred_element_type=jnp.float32)


def route_kernel(in_ref, out_ref, best_ref):
    count = in_ref.shape[0] // SLOT
    boxes = 2 * count
    header = in_ref[pl.ds(20, count, stride=SLOT), :]
    best = jnp.max(jnp.where(lane_index(header.shape) == 6, header, 0.0), axis=0, keepdims=True)
    best = jnp.max(best, axis=1, keepdims=True)
    best_ref[...] = jnp.broadcast_to(best.reshape(1, 1, 1), best_ref.shape)
    both = jnp.concatenate([header, pltpu.roll(header, LANES - 1, 1)], axis=0)
    target = jnp.broadcast_to(jnp.transpose(both)[0:1, :], (boxes, boxes))
    index = lax.broadcasted_iota(jnp.int32, (boxes, boxes), 0).astype(jnp.float32)

    def beside(first, second):
        rows = jnp.concatenate([header[:, first : first + 1], header[:, second : second + 1]], axis=0)
        return jnp.broadcast_to(rows, (boxes, boxes))

    columns = []
    for row in range(ROWS):
        columns.append(
            jnp.concatenate(
                [in_ref[pl.ds(ROWS * box + row, count, stride=SLOT), :] for box in range(2)], axis=0
            )
        )
    lane2 = lane_index((boxes, LANES))
    last = jnp.zeros((boxes, LANES), jnp.float32)
    first = jnp.zeros((boxes, LANES), jnp.float32)
    for v in range(5):
        mine = (lane2 >= 16 * v) & (lane2 < 16 * (v + 1))
        last = jnp.where(mine, pltpu.roll(columns[2 * v + 1], 16 * (v + 1), 1), last)
        first = jnp.where(mine, pltpu.roll(columns[2 * v], 16 * v, 1) if v else columns[0], first)
    placed = gather_rows(index == target, three_parts(jnp.concatenate(columns, axis=1)))
    below = gather_rows(beside(2, 4) == target, three_parts(last))
    above = gather_rows(beside(3, 5) == target, three_parts(first))
    for box in range(2):
        rows = slice(count * box, count * (box + 1))
        for row in range(ROWS):
            out_ref[pl.ds(ROWS * box + row, count, stride=SLOT), :] = placed[rows, LANES * row : LANES * (row + 1)]
        out_ref[pl.ds(20 + box, count, stride=SLOT), :] = below[rows]
        out_ref[pl.ds(22 + box, count, stride=SLOT), :] = above[rows]


def advance_kernel(pick_ref, in_ref, before_ref, after_ref, best_ref, out_ref):
    count = in_ref.shape[0] // SLOT

    def rows_of(row):
        return in_ref[pl.ds(row, count, stride=SLOT), :]

    def pick(box, face):
        return pick_ref[0:1, 6 * box + face : 6 * box + face + 1]

    cell = [
        jnp.stack([rows_of(ROWS * box + 2 * v + half) for box in range(2) for half in range(2)]) for v in range(5)
    ]
    velocity, _, sound = primitives(cell)
    lane = lane_index(cell[0].shape)

    own = (in_ref[SLOT * (count - 1) : SLOT * count, :], in_ref[0:SLOT, :])
    other = (before_ref[...], after_ref[...])
    ghosts = []
    for face in range(2):
        for box in range(2):
            wanted = pick(box, face)
            rows = jnp.where(wanted >= 2.0, own[face], other[face])
            first = (wanted == 0.0) | (wanted == 2.0)
            ghosts.append(jnp.where(first, rows[0:ROWS], rows[ROWS : 2 * ROWS]))
    layer = lax.broadcasted_iota(jnp.int32, cell[0].shape, 1)
    below, above = [], []
    for v in range(5):

        def spread(rows):
            return jnp.stack([rows[box][2 * v + half : 2 * v + half + 1] for box in range(2) for half in range(2)])

        below.append(jnp.where(layer == 0, spread(ghosts[0:2]), pltpu.roll(cell[v], 1, 1)))
        above.append(jnp.where(layer == count - 1, spread(ghosts[2:4]), pltpu.roll(cell[v], count - 1, 1)))
    change = axis_change(cell, jnp.abs(velocity[0]) + sound, below, above, 0)

    ghost_low = [rows_of(20 + box) for box in range(2)]
    ghost_high = [rows_of(22 + box) for box in range(2)]
    below, above = [], []
    for v in range(5):
        low = [pltpu.roll(g, LANES - 16 * v, 1) if v else g for g in ghost_low]
        high = [pltpu.roll(g, 112 - 16 * v, 1) for g in ghost_high]
        rolled = pltpu.roll(cell[v], 16, 2)
        edge = jnp.stack([low[0], rolled[0], low[1], rolled[2]])
        below.append(jnp.where(lane < 16, edge, rolled))
        rolled = pltpu.roll(cell[v], LANES - 16, 2)
        edge = jnp.stack([rolled[1], high[0], rolled[3], high[1]])
        above.append(jnp.where(lane >= LANES - 16, edge, rolled))
    more = axis_change(cell, jnp.abs(velocity[1]) + sound, below, above, 1)
    change = [change[v] + more[v] for v in range(5)]

    deep = lane & 15
    below, above = [], []
    slots = [[pick(box, face) == 0.0 for box in range(2)] for face in (4, 5)]
    for v in range(5):
        wrapped = pltpu.roll(cell[v], LANES - 15, 2)
        edge = jnp.concatenate([jnp.where(slots[0][box], wrapped[0:2], wrapped[2:4]) for box in range(2)], axis=0)
        below.append(jnp.where(deep == 0, edge, pltpu.roll(cell[v], 1, 2)))
        wrapped = pltpu.roll(cell[v], 15, 2)
        edge = jnp.concatenate([jnp.where(slots[1][box], wrapped[0:2], wrapped[2:4]) for box in range(2)], axis=0)
        above.append(jnp.where(deep == 15, edge, pltpu.roll(cell[v], LANES - 1, 2)))
    more = axis_change(cell, jnp.abs(velocity[2]) + sound, below, above, 2)

    step = courant / jnp.max(best_ref[...], axis=0)
    for v in range(5):
        result = cell[v] - step[None] * (change[v] + more[v])
        for box in range(2):
            for half in range(2):
                out_ref[box, v, :, LANES * half : LANES * (half + 1)] = result[2 * box + half]


def local(state, new_slot, neighbours):
    count = lax.axis_size("curve")
    segs = lax.axis_size("seg")
    f32 = jnp.float32
    sent, pick = pl.pallas_call(
        pack_kernel,
        out_shape=(jax.ShapeDtypeStruct((SLOT * count, LANES), f32), jax.ShapeDtypeStruct((8, LANES), f32)),
        in_specs=[hbm, hbm, hbm],
        out_specs=(vmem, vmem),
        scratch_shapes=[
            pltpu.SMEM(new_slot.shape, jnp.int32),
            pltpu.SMEM(neighbours.shape, jnp.int32),
            pltpu.VMEM(state.shape, f32),
            pltpu.SemaphoreType.DMA((3,)),
        ],
        name="pack",
    )(new_slot, neighbours, state)
    met = lax.all_to_all(sent.reshape(count, SLOT, LANES), "curve", 0, 0, tiled=True)
    routed, best = pl.pallas_call(
        route_kernel,
        out_shape=(
            jax.ShapeDtypeStruct((SLOT * count, LANES), f32),
            jax.ShapeDtypeStruct((segs, 1, LANES), f32),
        ),
        in_specs=[vmem],
        out_specs=(vmem, vmem),
        compiler_params=params,
        name="route",
    )(met.reshape(SLOT * count, LANES))
    moved = lax.all_to_all(routed.reshape(count, SLOT, LANES), "curve", 0, 0, tiled=True)
    up = [(i, (i + 1) % segs) for i in range(segs)]
    down = [(j, i) for i, j in up]
    before = lax.ppermute(moved[count - 1], "seg", up)
    after = lax.ppermute(moved[0], "seg", down)
    best, before, after = lax.optimization_barrier((best, before, after))
    best = lax.all_to_all(best, "seg", 0, 0, tiled=True)
    return pl.pallas_call(
        advance_kernel,
        out_shape=jax.ShapeDtypeStruct(state.shape, f32),
        in_specs=[vmem] * 5,
        out_specs=vmem,
        compiler_params=params,
        name="advance",
    )(pick, moved.reshape(SLOT * count, LANES), before, after, best)


def solution(mesh):
    placed = P(("seg", "curve"))
    return jax.shard_map(
        local, mesh=mesh, in_specs=(placed, placed, placed), out_specs=placed, check_vma=False
    )
```

```python
import jax
import jax.numpy as jnp
from jax import lax
from jax.experimental import pallas as pl
from jax.experimental.pallas import tpu as pltpu
from jax.sharding import PartitionSpec as P

gamma_ratio = 1.4
courant = 0.3

LANES = 128
ROWS = 10
SLOT = 24

vmem = pl.BlockSpec(memory_space=pltpu.VMEM)
hbm = pl.BlockSpec(memory_space=pltpu.HBM)
params = pltpu.CompilerParams(vmem_limit_bytes=16 * 2**20)


def lane_index(shape):
    return lax.broadcasted_iota(jnp.int32, shape, len(shape) - 1)


def primitives(cell):
    inverse = 1.0 / cell[0]
    velocity = [cell[1 + d] * inverse for d in range(3)]
    kinetic = 0.5 * (cell[1] * velocity[0] + cell[2] * velocity[1] + cell[3] * velocity[2])
    pressure = (gamma_ratio - 1.0) * (cell[4] - kinetic)
    sound = jnp.sqrt(gamma_ratio * pressure * inverse)
    return velocity, pressure, sound


def side(cell, axis_num):
    velocity, pressure, sound = primitives(cell)
    along = velocity[axis_num]
    flux = [cell[1 + axis_num]]
    for d in range(3):
        term = cell[1 + d] * along
        flux.append(term + pressure if d == axis_num else term)
    flux.append((cell[4] + pressure) * along)
    return flux, jnp.abs(along) + sound


def axis_change(cell, speed, below, above, axis_num):
    flux_below, speed_below = side(below, axis_num)
    flux_above, speed_above = side(above, axis_num)
    speed_below = jnp.maximum(speed, speed_below)
    speed_above = jnp.maximum(speed, speed_above)
    return [
        0.5 * (flux_above[v] - flux_below[v])
        - 0.5 * (speed_above * (above[v] - cell[v]) - speed_below * (cell[v] - below[v]))
        for v in range(5)
    ]


def pack_kernel(slot_hbm, near_hbm, state_hbm, out_ref, pick_ref, slot_ref, near_ref, state_ref, sems):
    copies = [
        pltpu.make_async_copy(source, target, sems.at[i])
        for i, (source, target) in enumerate(
            (
                (state_hbm.at[0], state_ref.at[0]),
                (state_hbm.at[1], state_ref.at[1]),
                (slot_hbm, slot_ref),
                (near_hbm, near_ref),
            )
        )
    ]
    for copy in copies:
        copy.start()
    count = out_ref.shape[0] // SLOT
    boxes = 2 * count
    best = None
    for box in range(2):
        copies[box].wait()
        cell = [state_ref[box, v] for v in range(5)]
        for v in range(5):
            for half in range(2):
                row = ROWS * box + 2 * v + half
                out_ref[pl.ds(row, count, stride=SLOT), :] = cell[v][:, LANES * half : LANES * (half + 1)]
        velocity, _, sound = primitives(cell)
        largest = jnp.maximum(jnp.maximum(jnp.abs(velocity[0]), jnp.abs(velocity[1])), jnp.abs(velocity[2]))
        speed = largest + sound
        best = speed if best is None else jnp.maximum(best, speed)
    best = jnp.max(jnp.max(best, axis=0, keepdims=True), axis=1, keepdims=True)

    def place(index):
        local = lax.rem(index, boxes)
        return lax.rem(local, 2) * count + lax.div(local, 2)

    copies[2].wait()
    copies[3].wait()
    values = [place(slot_ref[0]), place(slot_ref[1])]
    for box in range(2):
        values += [place(near_ref[box, 2]), place(near_ref[box, 3])]
    lane = lane_index((count, LANES))
    header = jnp.where(lane == 6, jnp.broadcast_to(best, lane.shape), 0.0)
    for position, value in enumerate(values):
        header = jnp.where(lane == position, value.astype(jnp.float32), header)
    out_ref[pl.ds(20, count, stride=SLOT), :] = header
    for row in range(21, SLOT):
        out_ref[pl.ds(row, count, stride=SLOT), :] = jnp.zeros((count, LANES), jnp.float32)

    segment = lax.axis_index("seg")
    lane = lane_index(pick_ref.shape)
    picks = jnp.zeros(pick_ref.shape, jnp.float32)
    for box in range(2):
        for face in (0, 1, 4, 5):
            index = near_ref[box, face]
            value = lax.rem(index, 2)
            if face < 2:
                value = value + jnp.where(lax.div(index, boxes) == segment, 2, 0)
            picks = jnp.where(lane == 6 * box + face, value.astype(jnp.float32), picks)
    pick_ref[...] = picks


def three_parts(value):
    high = value.astype(jnp.bfloat16)
    rest = value - high.astype(jnp.float32)
    middle = rest.astype(jnp.bfloat16)
    low = (rest - middle.astype(jnp.float32)).astype(jnp.bfloat16)
    return jnp.concatenate([high, middle, low], axis=0)


def gather_rows(one_hot, parts):
    chosen = jnp.where(one_hot, 1.0, 0.0).astype(jnp.bfloat16)
    return jnp.dot(jnp.concatenate([chosen] * 3, axis=1), parts, preferred_element_type=jnp.float32)


def route_kernel(in_ref, out_ref, best_ref):
    count = in_ref.shape[0] // SLOT
    boxes = 2 * count
    header = in_ref[pl.ds(20, count, stride=SLOT), :]
    best = jnp.max(jnp.where(lane_index(header.shape) == 6, header, 0.0), axis=0, keepdims=True)
    best = jnp.max(best, axis=1, keepdims=True)
    best_ref[...] = jnp.broadcast_to(best.reshape(1, 1, 1), best_ref.shape)
    both = jnp.concatenate([header, pltpu.roll(header, LANES - 1, 1)], axis=0)
    target = jnp.broadcast_to(jnp.transpose(both)[0:1, :], (boxes, boxes))
    index = lax.broadcasted_iota(jnp.int32, (boxes, boxes), 0).astype(jnp.float32)

    def beside(first, second):
        rows = jnp.concatenate([header[:, first : first + 1], header[:, second : second + 1]], axis=0)
        return jnp.broadcast_to(rows, (boxes, boxes))

    columns = []
    for row in range(ROWS):
        columns.append(
            jnp.concatenate(
                [in_ref[pl.ds(ROWS * box + row, count, stride=SLOT), :] for box in range(2)], axis=0
            )
        )
    lane2 = lane_index((boxes, LANES))
    last = jnp.zeros((boxes, LANES), jnp.float32)
    first = jnp.zeros((boxes, LANES), jnp.float32)
    for v in range(5):
        mine = (lane2 >= 16 * v) & (lane2 < 16 * (v + 1))
        last = jnp.where(mine, pltpu.roll(columns[2 * v + 1], 16 * (v + 1), 1), last)
        first = jnp.where(mine, pltpu.roll(columns[2 * v], 16 * v, 1) if v else columns[0], first)
    placed = gather_rows(index == target, three_parts(jnp.concatenate(columns, axis=1)))
    below = gather_rows(beside(2, 4) == target, three_parts(last))
    above = gather_rows(beside(3, 5) == target, three_parts(first))
    for box in range(2):
        rows = slice(count * box, count * (box + 1))
        for row in range(ROWS):
            out_ref[pl.ds(ROWS * box + row, count, stride=SLOT), :] = placed[rows, LANES * row : LANES * (row + 1)]
        out_ref[pl.ds(20 + box, count, stride=SLOT), :] = below[rows]
        out_ref[pl.ds(22 + box, count, stride=SLOT), :] = above[rows]


def advance_kernel(pick_ref, in_ref, before_ref, after_ref, best_ref, out_ref):
    count = in_ref.shape[0] // SLOT

    def rows_of(row):
        return in_ref[pl.ds(row, count, stride=SLOT), :]

    def pick(box, face):
        return pick_ref[0:1, 6 * box + face : 6 * box + face + 1]

    cell = [
        jnp.stack([rows_of(ROWS * box + 2 * v + half) for box in range(2) for half in range(2)]) for v in range(5)
    ]
    velocity, _, sound = primitives(cell)
    lane = lane_index(cell[0].shape)

    own = (in_ref[SLOT * (count - 1) : SLOT * count, :], in_ref[0:SLOT, :])
    other = (before_ref[...], after_ref[...])
    ghosts = []
    for face in range(2):
        for box in range(2):
            wanted = pick(box, face)
            rows = jnp.where(wanted >= 2.0, own[face], other[face])
            first = (wanted == 0.0) | (wanted == 2.0)
            ghosts.append(jnp.where(first, rows[0:ROWS], rows[ROWS : 2 * ROWS]))
    layer = lax.broadcasted_iota(jnp.int32, cell[0].shape, 1)
    below, above = [], []
    for v in range(5):

        def spread(rows):
            return jnp.stack([rows[box][2 * v + half : 2 * v + half + 1] for box in range(2) for half in range(2)])

        below.append(jnp.where(layer == 0, spread(ghosts[0:2]), pltpu.roll(cell[v], 1, 1)))
        above.append(jnp.where(layer == count - 1, spread(ghosts[2:4]), pltpu.roll(cell[v], count - 1, 1)))
    change = axis_change(cell, jnp.abs(velocity[0]) + sound, below, above, 0)

    ghost_low = [rows_of(20 + box) for box in range(2)]
    ghost_high = [rows_of(22 + box) for box in range(2)]
    below, above = [], []
    for v in range(5):
        low = [pltpu.roll(g, LANES - 16 * v, 1) if v else g for g in ghost_low]
        high = [pltpu.roll(g, 112 - 16 * v, 1) for g in ghost_high]
        rolled = pltpu.roll(cell[v], 16, 2)
        edge = jnp.stack([low[0], rolled[0], low[1], rolled[2]])
        below.append(jnp.where(lane < 16, edge, rolled))
        rolled = pltpu.roll(cell[v], LANES - 16, 2)
        edge = jnp.stack([rolled[1], high[0], rolled[3], high[1]])
        above.append(jnp.where(lane >= LANES - 16, edge, rolled))
    more = axis_change(cell, jnp.abs(velocity[1]) + sound, below, above, 1)
    change = [change[v] + more[v] for v in range(5)]

    deep = lane & 15
    below, above = [], []
    slots = [[pick(box, face) == 0.0 for box in range(2)] for face in (4, 5)]
    for v in range(5):
        wrapped = pltpu.roll(cell[v], LANES - 15, 2)
        edge = jnp.concatenate([jnp.where(slots[0][box], wrapped[0:2], wrapped[2:4]) for box in range(2)], axis=0)
        below.append(jnp.where(deep == 0, edge, pltpu.roll(cell[v], 1, 2)))
        wrapped = pltpu.roll(cell[v], 15, 2)
        edge = jnp.concatenate([jnp.where(slots[1][box], wrapped[0:2], wrapped[2:4]) for box in range(2)], axis=0)
        above.append(jnp.where(deep == 15, edge, pltpu.roll(cell[v], LANES - 1, 2)))
    more = axis_change(cell, jnp.abs(velocity[2]) + sound, below, above, 2)

    step = courant / jnp.max(best_ref[...], axis=0)
    for v in range(5):
        result = cell[v] - step[None] * (change[v] + more[v])
        for box in range(2):
            for half in range(2):
                out_ref[box, v, :, LANES * half : LANES * (half + 1)] = result[2 * box + half]


def local(state, new_slot, neighbours):
    count = lax.axis_size("curve")
    segs = lax.axis_size("seg")
    f32 = jnp.float32
    sent, pick = pl.pallas_call(
        pack_kernel,
        out_shape=(jax.ShapeDtypeStruct((SLOT * count, LANES), f32), jax.ShapeDtypeStruct((8, LANES), f32)),
        in_specs=[hbm, hbm, hbm],
        out_specs=(vmem, vmem),
        scratch_shapes=[
            pltpu.SMEM(new_slot.shape, jnp.int32),
            pltpu.SMEM(neighbours.shape, jnp.int32),
            pltpu.VMEM(state.shape, f32),
            pltpu.SemaphoreType.DMA((4,)),
        ],
        name="pack",
    )(new_slot, neighbours, state)
    met = lax.all_to_all(sent.reshape(count, SLOT, LANES), "curve", 0, 0, tiled=True)
    routed, best = pl.pallas_call(
        route_kernel,
        out_shape=(
            jax.ShapeDtypeStruct((SLOT * count, LANES), f32),
            jax.ShapeDtypeStruct((segs, 1, LANES), f32),
        ),
        in_specs=[vmem],
        out_specs=(vmem, vmem),
        compiler_params=params,
        name="route",
    )(met.reshape(SLOT * count, LANES))
    moved = lax.all_to_all(routed.reshape(count, SLOT, LANES), "curve", 0, 0, tiled=True)
    up = [(i, (i + 1) % segs) for i in range(segs)]
    down = [(j, i) for i, j in up]
    before = lax.ppermute(moved[count - 1], "seg", up)
    after = lax.ppermute(moved[0], "seg", down)
    best = lax.all_to_all(best, "seg", 0, 0, tiled=True)
    return pl.pallas_call(
        advance_kernel,
        out_shape=jax.ShapeDtypeStruct(state.shape, f32),
        in_specs=[vmem] * 5,
        out_specs=vmem,
        compiler_params=params,
        name="advance",
    )(pick, moved.reshape(SLOT * count, LANES), before, after, best)


def solution(mesh):
    placed = P(("seg", "curve"))
    return jax.shard_map(
        local, mesh=mesh, in_specs=(placed, placed, placed), out_specs=placed, check_vma=False
    )
```

```python
import math

import jax
import jax.numpy as jnp
from jax import lax
from jax.experimental import pallas as pl
from jax.experimental.pallas import tpu as pltpu
from jax.sharding import Mesh, PartitionSpec as P

gamma_ratio = 1.4
courant = 0.3

LANES = 128
SEG = ("seg_x", "seg_z")
ROWS = 10
SLOT = 24

vmem = pl.BlockSpec(memory_space=pltpu.VMEM)
hbm = pl.BlockSpec(memory_space=pltpu.HBM)
params = pltpu.CompilerParams(vmem_limit_bytes=16 * 2**20)


def lane_index(shape):
    return lax.broadcasted_iota(jnp.int32, shape, len(shape) - 1)


def primitives(cell):
    inverse = 1.0 / cell[0]
    velocity = [cell[1 + d] * inverse for d in range(3)]
    kinetic = 0.5 * (cell[1] * velocity[0] + cell[2] * velocity[1] + cell[3] * velocity[2])
    pressure = (gamma_ratio - 1.0) * (cell[4] - kinetic)
    sound = jnp.sqrt(gamma_ratio * pressure * inverse)
    return velocity, pressure, sound


def side(cell, axis_num):
    velocity, pressure, sound = primitives(cell)
    along = velocity[axis_num]
    flux = [cell[1 + axis_num]]
    for d in range(3):
        term = cell[1 + d] * along
        flux.append(term + pressure if d == axis_num else term)
    flux.append((cell[4] + pressure) * along)
    return flux, jnp.abs(along) + sound


def axis_change(cell, speed, below, above, axis_num):
    flux_below, speed_below = side(below, axis_num)
    flux_above, speed_above = side(above, axis_num)
    speed_below = jnp.maximum(speed, speed_below)
    speed_above = jnp.maximum(speed, speed_above)
    return [
        0.5 * (flux_above[v] - flux_below[v])
        - 0.5 * (speed_above * (above[v] - cell[v]) - speed_below * (cell[v] - below[v]))
        for v in range(5)
    ]


def pack_kernel(slot_hbm, near_hbm, state_hbm, out_ref, pick_ref, slot_ref, near_ref, state_ref, sems):
    copies = [
        pltpu.make_async_copy(source, target, sems.at[i])
        for i, (source, target) in enumerate(
            (
                (state_hbm.at[0], state_ref.at[0]),
                (state_hbm.at[1], state_ref.at[1]),
                (slot_hbm, slot_ref),
                (near_hbm, near_ref),
            )
        )
    ]
    for copy in copies:
        copy.start()
    count = out_ref.shape[0] // SLOT
    boxes = 2 * count
    best = None
    for box in range(2):
        copies[box].wait()
        cell = [state_ref[box, v] for v in range(5)]
        for v in range(5):
            for half in range(2):
                row = ROWS * box + 2 * v + half
                out_ref[pl.ds(row, count, stride=SLOT), :] = cell[v][:, LANES * half : LANES * (half + 1)]
        velocity, _, sound = primitives(cell)
        largest = jnp.maximum(jnp.maximum(jnp.abs(velocity[0]), jnp.abs(velocity[1])), jnp.abs(velocity[2]))
        speed = largest + sound
        best = speed if best is None else jnp.maximum(best, speed)
    best = jnp.max(jnp.max(best, axis=0, keepdims=True), axis=1, keepdims=True)

    def place(index):
        local = lax.rem(index, boxes)
        return lax.rem(local, 2) * count + lax.div(local, 2)

    copies[2].wait()
    copies[3].wait()
    values = [place(slot_ref[0]), place(slot_ref[1])]
    for box in range(2):
        values += [place(near_ref[box, 2]), place(near_ref[box, 3])]
    lane = lane_index((count, LANES))
    header = jnp.where(lane == 6, jnp.broadcast_to(best, lane.shape), 0.0)
    for position, value in enumerate(values):
        header = jnp.where(lane == position, value.astype(jnp.float32), header)
    out_ref[pl.ds(20, count, stride=SLOT), :] = header
    for row in range(21, SLOT):
        out_ref[pl.ds(row, count, stride=SLOT), :] = jnp.zeros((count, LANES), jnp.float32)

    segment = lax.axis_index(SEG)
    lane = lane_index(pick_ref.shape)
    picks = jnp.zeros(pick_ref.shape, jnp.float32)
    for box in range(2):
        for face in (0, 1, 4, 5):
            index = near_ref[box, face]
            value = lax.rem(index, 2)
            if face < 2:
                value = value + jnp.where(lax.div(index, boxes) == segment, 2, 0)
            picks = jnp.where(lane == 6 * box + face, value.astype(jnp.float32), picks)
    pick_ref[...] = picks


def three_parts(value):
    high = value.astype(jnp.bfloat16)
    rest = value - high.astype(jnp.float32)
    middle = rest.astype(jnp.bfloat16)
    low = (rest - middle.astype(jnp.float32)).astype(jnp.bfloat16)
    return jnp.concatenate([high, middle, low], axis=0)


def gather_rows(one_hot, parts):
    chosen = jnp.where(one_hot, 1.0, 0.0).astype(jnp.bfloat16)
    return jnp.dot(jnp.concatenate([chosen] * 3, axis=1), parts, preferred_element_type=jnp.float32)


def route_kernel(in_ref, out_ref, best_ref):
    count = in_ref.shape[0] // SLOT
    boxes = 2 * count
    header = in_ref[pl.ds(20, count, stride=SLOT), :]
    best = jnp.max(jnp.where(lane_index(header.shape) == 6, header, 0.0), axis=0, keepdims=True)
    best = jnp.max(best, axis=1, keepdims=True)
    best_ref[...] = jnp.broadcast_to(best.reshape(1, 1, 1), best_ref.shape)
    both = jnp.concatenate([header, pltpu.roll(header, LANES - 1, 1)], axis=0)
    target = jnp.broadcast_to(jnp.transpose(both)[0:1, :], (boxes, boxes))
    index = lax.broadcasted_iota(jnp.int32, (boxes, boxes), 0).astype(jnp.float32)

    def beside(first, second):
        rows = jnp.concatenate([header[:, first : first + 1], header[:, second : second + 1]], axis=0)
        return jnp.broadcast_to(rows, (boxes, boxes))

    columns = []
    for row in range(ROWS):
        columns.append(
            jnp.concatenate(
                [in_ref[pl.ds(ROWS * box + row, count, stride=SLOT), :] for box in range(2)], axis=0
            )
        )
    lane2 = lane_index((boxes, LANES))
    last = jnp.zeros((boxes, LANES), jnp.float32)
    first = jnp.zeros((boxes, LANES), jnp.float32)
    for v in range(5):
        mine = (lane2 >= 16 * v) & (lane2 < 16 * (v + 1))
        last = jnp.where(mine, pltpu.roll(columns[2 * v + 1], 16 * (v + 1), 1), last)
        first = jnp.where(mine, pltpu.roll(columns[2 * v], 16 * v, 1) if v else columns[0], first)
    placed = gather_rows(index == target, three_parts(jnp.concatenate(columns, axis=1)))
    below = gather_rows(beside(2, 4) == target, three_parts(last))
    above = gather_rows(beside(3, 5) == target, three_parts(first))
    for box in range(2):
        rows = slice(count * box, count * (box + 1))
        for row in range(ROWS):
            out_ref[pl.ds(ROWS * box + row, count, stride=SLOT), :] = placed[rows, LANES * row : LANES * (row + 1)]
        out_ref[pl.ds(20 + box, count, stride=SLOT), :] = below[rows]
        out_ref[pl.ds(22 + box, count, stride=SLOT), :] = above[rows]


def peak_kernel(in_ref, out_ref):
    best = jnp.max(in_ref[...], axis=0, keepdims=True)
    out_ref[...] = jnp.broadcast_to(best, out_ref.shape)


def change_kernel(pick_ref, in_ref, before_ref, after_ref, out_ref):
    count = in_ref.shape[0] // SLOT

    def rows_of(row):
        return in_ref[pl.ds(row, count, stride=SLOT), :]

    def pick(box, face):
        return pick_ref[0:1, 6 * box + face : 6 * box + face + 1]

    cell = [
        jnp.stack([rows_of(ROWS * box + 2 * v + half) for box in range(2) for half in range(2)]) for v in range(5)
    ]
    velocity, _, sound = primitives(cell)
    lane = lane_index(cell[0].shape)

    own = (in_ref[SLOT * (count - 1) : SLOT * count, :], in_ref[0:SLOT, :])
    other = (before_ref[...], after_ref[...])
    ghosts = []
    for face in range(2):
        for box in range(2):
            wanted = pick(box, face)
            rows = jnp.where(wanted >= 2.0, own[face], other[face])
            first = (wanted == 0.0) | (wanted == 2.0)
            ghosts.append(jnp.where(first, rows[0:ROWS], rows[ROWS : 2 * ROWS]))
    layer = lax.broadcasted_iota(jnp.int32, cell[0].shape, 1)
    below, above = [], []
    for v in range(5):

        def spread(rows):
            return jnp.stack([rows[box][2 * v + half : 2 * v + half + 1] for box in range(2) for half in range(2)])

        below.append(jnp.where(layer == 0, spread(ghosts[0:2]), pltpu.roll(cell[v], 1, 1)))
        above.append(jnp.where(layer == count - 1, spread(ghosts[2:4]), pltpu.roll(cell[v], count - 1, 1)))
    change = axis_change(cell, jnp.abs(velocity[0]) + sound, below, above, 0)

    ghost_low = [rows_of(20 + box) for box in range(2)]
    ghost_high = [rows_of(22 + box) for box in range(2)]
    below, above = [], []
    for v in range(5):
        low = [pltpu.roll(g, LANES - 16 * v, 1) if v else g for g in ghost_low]
        high = [pltpu.roll(g, 112 - 16 * v, 1) for g in ghost_high]
        rolled = pltpu.roll(cell[v], 16, 2)
        edge = jnp.stack([low[0], rolled[0], low[1], rolled[2]])
        below.append(jnp.where(lane < 16, edge, rolled))
        rolled = pltpu.roll(cell[v], LANES - 16, 2)
        edge = jnp.stack([rolled[1], high[0], rolled[3], high[1]])
        above.append(jnp.where(lane >= LANES - 16, edge, rolled))
    more = axis_change(cell, jnp.abs(velocity[1]) + sound, below, above, 1)
    change = [change[v] + more[v] for v in range(5)]

    deep = lane & 15
    below, above = [], []
    slots = [[pick(box, face) == 0.0 for box in range(2)] for face in (4, 5)]
    for v in range(5):
        wrapped = pltpu.roll(cell[v], LANES - 15, 2)
        edge = jnp.concatenate([jnp.where(slots[0][box], wrapped[0:2], wrapped[2:4]) for box in range(2)], axis=0)
        below.append(jnp.where(deep == 0, edge, pltpu.roll(cell[v], 1, 2)))
        wrapped = pltpu.roll(cell[v], 15, 2)
        edge = jnp.concatenate([jnp.where(slots[1][box], wrapped[0:2], wrapped[2:4]) for box in range(2)], axis=0)
        above.append(jnp.where(deep == 15, edge, pltpu.roll(cell[v], LANES - 1, 2)))
    more = axis_change(cell, jnp.abs(velocity[2]) + sound, below, above, 2)

    for v in range(5):
        out_ref[v] = change[v] + more[v]


def finish_kernel(in_ref, change_ref, best_ref, out_ref):
    count = in_ref.shape[0] // SLOT
    step = courant / jnp.max(best_ref[...], axis=0)
    for box in range(2):
        for v in range(5):
            for half in range(2):
                cell = in_ref[pl.ds(ROWS * box + 2 * v + half, count, stride=SLOT), :]
                columns = slice(LANES * half, LANES * (half + 1))
                out_ref[box, v, :, columns] = cell - step * change_ref[v, 2 * box + half]


def local(state, new_slot, neighbours):
    count = lax.axis_size("curve")
    along_x, along_z = (lax.axis_size(axis) for axis in SEG)
    segs = along_x * along_z
    f32 = jnp.float32
    sent, pick = pl.pallas_call(
        pack_kernel,
        out_shape=(jax.ShapeDtypeStruct((SLOT * count, LANES), f32), jax.ShapeDtypeStruct((8, LANES), f32)),
        in_specs=[hbm, hbm, hbm],
        out_specs=(vmem, vmem),
        scratch_shapes=[
            pltpu.SMEM(new_slot.shape, jnp.int32),
            pltpu.SMEM(neighbours.shape, jnp.int32),
            pltpu.VMEM(state.shape, f32),
            pltpu.SemaphoreType.DMA((4,)),
        ],
        name="pack",
    )(new_slot, neighbours, state)
    met = lax.all_to_all(sent.reshape(count, SLOT, LANES), "curve", 0, 0, tiled=True)
    routed, best = pl.pallas_call(
        route_kernel,
        out_shape=(
            jax.ShapeDtypeStruct((SLOT * count, LANES), f32),
            jax.ShapeDtypeStruct((along_z, 1, LANES), f32),
        ),
        in_specs=[vmem],
        out_specs=(vmem, vmem),
        compiler_params=params,
        name="route",
    )(met.reshape(SLOT * count, LANES))
    moved = lax.all_to_all(routed.reshape(count, SLOT, LANES), "curve", 0, 0, tiled=True)
    up = [(i, (i + 1) % segs) for i in range(segs)]
    down = [(j, i) for i, j in up]
    best = lax.all_to_all(best, SEG[1], 0, 0, tiled=True)
    before = lax.ppermute(moved[count - 1], SEG, up)
    after = lax.ppermute(moved[0], SEG, down)
    best = pl.pallas_call(
        peak_kernel,
        out_shape=jax.ShapeDtypeStruct((along_x, 1, LANES), f32),
        in_specs=[vmem],
        out_specs=vmem,
        compiler_params=params,
        name="peak",
    )(best)
    best = lax.all_to_all(best, SEG[0], 0, 0, tiled=True)
    moved = moved.reshape(SLOT * count, LANES)
    change = pl.pallas_call(
        change_kernel,
        out_shape=jax.ShapeDtypeStruct((5, 4, count, LANES), f32),
        in_specs=[vmem] * 4,
        out_specs=vmem,
        compiler_params=params,
        name="change",
    )(pick, moved, before, after)
    return pl.pallas_call(
        finish_kernel,
        out_shape=jax.ShapeDtypeStruct(state.shape, f32),
        in_specs=[vmem] * 3,
        out_specs=vmem,
        compiler_params=params,
        name="finish",
    )(moved, change, best)


def solution(mesh):
    segs, count = mesh.devices.shape
    side_x = math.isqrt(segs)
    grid = Mesh(mesh.devices.reshape(side_x, segs // side_x, count), SEG + ("curve",))
    placed = P(SEG + ("curve",))
    return jax.shard_map(
        local, mesh=grid, in_specs=(placed, placed, placed), out_specs=placed, check_vma=False
    )
```

```python
import jax
import jax.numpy as jnp
from jax import lax
from jax.experimental import pallas as pl
from jax.experimental.pallas import tpu as pltpu
from jax.sharding import PartitionSpec as P

gamma_ratio = 1.4
courant = 0.3

LANES = 128
ROWS = 10
SLOT = 24
TOP = 96

vmem = pl.BlockSpec(memory_space=pltpu.VMEM)
hbm = pl.BlockSpec(memory_space=pltpu.HBM)
params = pltpu.CompilerParams(vmem_limit_bytes=16 * 2**20)


def lane_index(shape):
    return lax.broadcasted_iota(jnp.int32, shape, len(shape) - 1)


def primitives(cell):
    inverse = 1.0 / cell[0]
    velocity = [cell[1 + d] * inverse for d in range(3)]
    kinetic = 0.5 * (cell[1] * velocity[0] + cell[2] * velocity[1] + cell[3] * velocity[2])
    pressure = (gamma_ratio - 1.0) * (cell[4] - kinetic)
    sound = jnp.sqrt(gamma_ratio * pressure * inverse)
    return velocity, pressure, sound


def side(cell, axis_num):
    velocity, pressure, sound = primitives(cell)
    along = velocity[axis_num]
    flux = [cell[1 + axis_num]]
    for d in range(3):
        term = cell[1 + d] * along
        flux.append(term + pressure if d == axis_num else term)
    flux.append((cell[4] + pressure) * along)
    return flux, jnp.abs(along) + sound


def axis_change(cell, speed, below, above, axis_num):
    flux_below, speed_below = side(below, axis_num)
    flux_above, speed_above = side(above, axis_num)
    speed_below = jnp.maximum(speed, speed_below)
    speed_above = jnp.maximum(speed, speed_above)
    return [
        0.5 * (flux_above[v] - flux_below[v])
        - 0.5 * (speed_above * (above[v] - cell[v]) - speed_below * (cell[v] - below[v]))
        for v in range(5)
    ]


def pack_kernel(slot_hbm, near_hbm, state_hbm, out_ref, pick_ref, slot_ref, near_ref, state_ref, sems):
    copies = [
        pltpu.make_async_copy(source, target, sems.at[i])
        for i, (source, target) in enumerate(
            (
                (state_hbm.at[0], state_ref.at[0]),
                (state_hbm.at[1], state_ref.at[1]),
                (slot_hbm, slot_ref),
                (near_hbm, near_ref),
            )
        )
    ]
    for copy in copies:
        copy.start()
    count = out_ref.shape[0] // SLOT
    boxes = 2 * count
    best = None
    for box in range(2):
        copies[box].wait()
        cell = [state_ref[box, v] for v in range(5)]
        for v in range(5):
            for half in range(2):
                row = ROWS * box + 2 * v + half
                out_ref[pl.ds(row, count, stride=SLOT), :] = cell[v][:, LANES * half : LANES * (half + 1)]
        velocity, _, sound = primitives(cell)
        largest = jnp.maximum(jnp.maximum(jnp.abs(velocity[0]), jnp.abs(velocity[1])), jnp.abs(velocity[2]))
        speed = largest + sound
        best = speed if best is None else jnp.maximum(best, speed)
    best = jnp.max(jnp.max(best, axis=0, keepdims=True), axis=1, keepdims=True)

    def place(index):
        local = lax.rem(index, boxes)
        return lax.rem(local, 2) * count + lax.div(local, 2)

    copies[2].wait()
    copies[3].wait()
    values = [place(slot_ref[0]), place(slot_ref[1])]
    for box in range(2):
        values += [place(near_ref[box, 2]), place(near_ref[box, 3])]
    lane = lane_index((count, LANES))
    header = jnp.where(lane == 6, jnp.broadcast_to(best, lane.shape), 0.0)
    for position, value in enumerate(values):
        header = jnp.where(lane == position, value.astype(jnp.float32), header)
    out_ref[pl.ds(20, count, stride=SLOT), :] = header
    for row in range(21, SLOT):
        out_ref[pl.ds(row, count, stride=SLOT), :] = jnp.zeros((count, LANES), jnp.float32)

    segment = lax.axis_index("seg")
    lane = lane_index(pick_ref.shape)
    picks = jnp.zeros(pick_ref.shape, jnp.float32)
    for box in range(2):
        for face in (0, 1, 4, 5):
            index = near_ref[box, face]
            value = lax.rem(index, 2)
            if face < 2:
                value = value + jnp.where(lax.div(index, boxes) == segment, 2, 0)
            picks = jnp.where(lane == 6 * box + face, value.astype(jnp.float32), picks)
    pick_ref[...] = picks


def peak_kernel(in_ref, out_ref):
    count = in_ref.shape[0] // SLOT
    header = in_ref[pl.ds(20, count, stride=SLOT), :]
    best = jnp.max(jnp.where(lane_index(header.shape) == 6, header, 0.0), axis=0, keepdims=True)
    out_ref[...] = jnp.broadcast_to(jnp.max(best, axis=1, keepdims=True), out_ref.shape)


def three_parts(value):
    high = value.astype(jnp.bfloat16)
    rest = value - high.astype(jnp.float32)
    middle = rest.astype(jnp.bfloat16)
    low = (rest - middle.astype(jnp.float32)).astype(jnp.bfloat16)
    return jnp.concatenate([high, middle, low], axis=0)


def gather_rows(one_hot, parts):
    chosen = jnp.where(one_hot, 1.0, 0.0).astype(jnp.bfloat16)
    return jnp.dot(jnp.concatenate([chosen] * 3, axis=1), parts, preferred_element_type=jnp.float32)


def route_kernel(in_ref, speed_ref, out_ref):
    count = in_ref.shape[0] // SLOT
    boxes = 2 * count
    header = in_ref[pl.ds(20, count, stride=SLOT), :]
    both = jnp.concatenate([header, pltpu.roll(header, LANES - 1, 1)], axis=0)
    target = jnp.broadcast_to(jnp.transpose(both)[0:1, :], (boxes, boxes))
    index = lax.broadcasted_iota(jnp.int32, (boxes, boxes), 0).astype(jnp.float32)

    def beside(first, second):
        rows = jnp.concatenate([header[:, first : first + 1], header[:, second : second + 1]], axis=0)
        return jnp.broadcast_to(rows, (boxes, boxes))

    columns = []
    for row in range(ROWS):
        columns.append(
            jnp.concatenate(
                [in_ref[pl.ds(ROWS * box + row, count, stride=SLOT), :] for box in range(2)], axis=0
            )
        )
    lane2 = lane_index((boxes, LANES))
    last = jnp.zeros((boxes, LANES), jnp.float32)
    first = jnp.zeros((boxes, LANES), jnp.float32)
    for v in range(5):
        mine = (lane2 >= 16 * v) & (lane2 < 16 * (v + 1))
        last = jnp.where(mine, pltpu.roll(columns[2 * v + 1], 16 * (v + 1), 1), last)
        first = jnp.where(mine, pltpu.roll(columns[2 * v], 16 * v, 1) if v else columns[0], first)
    placed = gather_rows(index == target, three_parts(jnp.concatenate(columns, axis=1)))
    below = gather_rows(beside(2, 4) == target, three_parts(last))
    above = gather_rows(beside(3, 5) == target, three_parts(first))
    below = jnp.where(lane2 >= TOP, speed_ref[0:1, :], below)
    for box in range(2):
        rows = slice(count * box, count * (box + 1))
        for row in range(ROWS):
            out_ref[pl.ds(ROWS * box + row, count, stride=SLOT), :] = placed[rows, LANES * row : LANES * (row + 1)]
        out_ref[pl.ds(20 + box, count, stride=SLOT), :] = below[rows]
        out_ref[pl.ds(22 + box, count, stride=SLOT), :] = above[rows]


def rows_of(ref, row):
    return ref[pl.ds(row, ref.shape[0] // SLOT, stride=SLOT), :]


def load_cells(ref):
    return [
        jnp.stack([rows_of(ref, ROWS * box + 2 * v + half) for box in range(2) for half in range(2)])
        for v in range(5)
    ]


def pick(ref, box, face):
    return ref[0:1, 6 * box + face : 6 * box + face + 1]


def faces_kernel(in_ref, first_ref, last_ref, speed_ref):
    count = in_ref.shape[0] // SLOT
    speeds = rows_of(in_ref, 20)
    best = jnp.max(jnp.where(lane_index(speeds.shape) >= TOP, speeds, 0.0), axis=0, keepdims=True)
    best = jnp.max(best, axis=1, keepdims=True)
    row = lax.broadcasted_iota(jnp.int32, first_ref.shape, 0)
    first_ref[...] = jnp.where(row < 2 * ROWS, in_ref[0:SLOT, :], best)
    last_ref[...] = jnp.where(row < 2 * ROWS, in_ref[SLOT * (count - 1) : SLOT * count, :], best)
    speed_ref[...] = jnp.broadcast_to(best, speed_ref.shape)


def planes_kernel(pick_ref, in_ref, out_ref):
    cell = load_cells(in_ref)
    velocity, _, sound = primitives(cell)
    lane = lane_index(cell[0].shape)

    ghost_low = [rows_of(in_ref, 20 + box) for box in range(2)]
    ghost_high = [rows_of(in_ref, 22 + box) for box in range(2)]
    below, above = [], []
    for v in range(5):
        low = [pltpu.roll(g, LANES - 16 * v, 1) if v else g for g in ghost_low]
        high = [pltpu.roll(g, 112 - 16 * v, 1) for g in ghost_high]
        rolled = pltpu.roll(cell[v], 16, 2)
        edge = jnp.stack([low[0], rolled[0], low[1], rolled[2]])
        below.append(jnp.where(lane < 16, edge, rolled))
        rolled = pltpu.roll(cell[v], LANES - 16, 2)
        edge = jnp.stack([rolled[1], high[0], rolled[3], high[1]])
        above.append(jnp.where(lane >= LANES - 16, edge, rolled))
    change = axis_change(cell, jnp.abs(velocity[1]) + sound, below, above, 1)

    deep = lane & 15
    below, above = [], []
    slots = [[pick(pick_ref, box, face) == 0.0 for box in range(2)] for face in (4, 5)]
    for v in range(5):
        wrapped = pltpu.roll(cell[v], LANES - 15, 2)
        edge = jnp.concatenate([jnp.where(slots[0][box], wrapped[0:2], wrapped[2:4]) for box in range(2)], axis=0)
        below.append(jnp.where(deep == 0, edge, pltpu.roll(cell[v], 1, 2)))
        wrapped = pltpu.roll(cell[v], 15, 2)
        edge = jnp.concatenate([jnp.where(slots[1][box], wrapped[0:2], wrapped[2:4]) for box in range(2)], axis=0)
        above.append(jnp.where(deep == 15, edge, pltpu.roll(cell[v], LANES - 1, 2)))
    more = axis_change(cell, jnp.abs(velocity[2]) + sound, below, above, 2)

    for v in range(5):
        out_ref[v] = change[v] + more[v]


def finish_kernel(pick_ref, in_ref, change_ref, before_ref, after_ref, speed_ref, beyond_ref, out_ref):
    count = in_ref.shape[0] // SLOT
    cell = load_cells(in_ref)
    velocity, _, sound = primitives(cell)
    own = (in_ref[SLOT * (count - 1) : SLOT * count, :], in_ref[0:SLOT, :])
    other = (before_ref[...], after_ref[...])
    ghosts = []
    for face in range(2):
        for box in range(2):
            wanted = pick(pick_ref, box, face)
            rows = jnp.where(wanted >= 2.0, own[face], other[face])
            first = (wanted == 0.0) | (wanted == 2.0)
            ghosts.append(jnp.where(first, rows[0:ROWS], rows[ROWS : 2 * ROWS]))
    layer = lax.broadcasted_iota(jnp.int32, cell[0].shape, 1)
    below, above = [], []
    for v in range(5):

        def spread(rows):
            return jnp.stack([rows[box][2 * v + half : 2 * v + half + 1] for box in range(2) for half in range(2)])

        below.append(jnp.where(layer == 0, spread(ghosts[0:2]), pltpu.roll(cell[v], 1, 1)))
        above.append(jnp.where(layer == count - 1, spread(ghosts[2:4]), pltpu.roll(cell[v], count - 1, 1)))
    change = axis_change(cell, jnp.abs(velocity[0]) + sound, below, above, 0)

    row = 2 * ROWS
    best = jnp.maximum(speed_ref[0:1, :], beyond_ref[0:1, :])
    best = jnp.maximum(best, jnp.maximum(before_ref[row : row + 1, :], after_ref[row : row + 1, :]))
    step = courant / best
    for v in range(5):
        result = cell[v] - step[None] * (change[v] + change_ref[v])
        for box in range(2):
            for half in range(2):
                out_ref[box, v, :, LANES * half : LANES * (half + 1)] = result[2 * box + half]


def local(state, new_slot, neighbours):
    count = lax.axis_size("curve")
    segs = lax.axis_size("seg")
    assert segs % 4 == 0 and segs <= 4 * count
    f32 = jnp.float32
    sent, pick = pl.pallas_call(
        pack_kernel,
        out_shape=(jax.ShapeDtypeStruct((SLOT * count, LANES), f32), jax.ShapeDtypeStruct((8, LANES), f32)),
        in_specs=[hbm, hbm, hbm],
        out_specs=(vmem, vmem),
        scratch_shapes=[
            pltpu.SMEM(new_slot.shape, jnp.int32),
            pltpu.SMEM(neighbours.shape, jnp.int32),
            pltpu.VMEM(state.shape, f32),
            pltpu.SemaphoreType.DMA((4,)),
        ],
        name="pack",
    )(new_slot, neighbours, state)
    met = lax.all_to_all(sent.reshape(count, SLOT, LANES), "curve", 0, 0, tiled=True)
    met = met.reshape(SLOT * count, LANES)
    speed = pl.pallas_call(
        peak_kernel,
        out_shape=jax.ShapeDtypeStruct((8, LANES), f32),
        in_specs=[vmem],
        out_specs=vmem,
        compiler_params=params,
        name="peak",
    )(met)
    spread = [((s + 4 * c) % segs * count + c, s * count + c) for s in range(segs) for c in range(count)]
    speed = lax.ppermute(speed, ("seg", "curve"), spread)
    routed = pl.pallas_call(
        route_kernel,
        out_shape=jax.ShapeDtypeStruct((SLOT * count, LANES), f32),
        in_specs=[vmem, vmem],
        out_specs=vmem,
        compiler_params=params,
        name="route",
    )(met, speed)
    moved = lax.all_to_all(routed.reshape(count, SLOT, LANES), "curve", 0, 0, tiled=True)
    moved = moved.reshape(SLOT * count, LANES)
    first, last, speed = pl.pallas_call(
        faces_kernel,
        out_shape=(
            jax.ShapeDtypeStruct((SLOT, LANES), f32),
            jax.ShapeDtypeStruct((SLOT, LANES), f32),
            jax.ShapeDtypeStruct((8, LANES), f32),
        ),
        in_specs=[vmem],
        out_specs=(vmem, vmem, vmem),
        compiler_params=params,
        name="faces",
    )(moved)
    before = lax.ppermute(last, "seg", [(i, (i + 1) % segs) for i in range(segs)])
    after = lax.ppermute(first, "seg", [((i + 1) % segs, i) for i in range(segs)])
    beyond = lax.ppermute(speed, "seg", [((i + 2) % segs, i) for i in range(segs)])
    change = pl.pallas_call(
        planes_kernel,
        out_shape=jax.ShapeDtypeStruct((5, 4, count, LANES), f32),
        in_specs=[vmem, vmem],
        out_specs=vmem,
        compiler_params=params,
        name="planes",
    )(pick, moved)
    return pl.pallas_call(
        finish_kernel,
        out_shape=jax.ShapeDtypeStruct(state.shape, f32),
        in_specs=[vmem] * 7,
        out_specs=vmem,
        compiler_params=params,
        name="finish",
    )(pick, moved, change, before, after, speed, beyond)


def solution(mesh):
    placed = P(("seg", "curve"))
    return jax.shard_map(
        local, mesh=mesh, in_specs=(placed, placed, placed), out_specs=placed, check_vma=False
    )
```

```python
import math

import jax
import jax.numpy as jnp
from jax import lax
from jax.experimental import pallas as pl
from jax.experimental.pallas import tpu as pltpu
from jax.sharding import Mesh, PartitionSpec as P

gamma_ratio = 1.4
courant = 0.3

LANES = 128
SEG = ("seg_x", "seg_z")
ROWS = 10
SLOT = 24

vmem = pl.BlockSpec(memory_space=pltpu.VMEM)
hbm = pl.BlockSpec(memory_space=pltpu.HBM)
params = pltpu.CompilerParams(vmem_limit_bytes=16 * 2**20)


def lane_index(shape):
    return lax.broadcasted_iota(jnp.int32, shape, len(shape) - 1)


def primitives(cell):
    inverse = 1.0 / cell[0]
    velocity = [cell[1 + d] * inverse for d in range(3)]
    kinetic = 0.5 * (cell[1] * velocity[0] + cell[2] * velocity[1] + cell[3] * velocity[2])
    pressure = (gamma_ratio - 1.0) * (cell[4] - kinetic)
    sound = jnp.sqrt(gamma_ratio * pressure * inverse)
    return velocity, pressure, sound


def side(cell, axis_num):
    velocity, pressure, sound = primitives(cell)
    along = velocity[axis_num]
    flux = [cell[1 + axis_num]]
    for d in range(3):
        term = cell[1 + d] * along
        flux.append(term + pressure if d == axis_num else term)
    flux.append((cell[4] + pressure) * along)
    return flux, jnp.abs(along) + sound


def axis_change(cell, speed, below, above, axis_num):
    flux_below, speed_below = side(below, axis_num)
    flux_above, speed_above = side(above, axis_num)
    speed_below = jnp.maximum(speed, speed_below)
    speed_above = jnp.maximum(speed, speed_above)
    return [
        0.5 * (flux_above[v] - flux_below[v])
        - 0.5 * (speed_above * (above[v] - cell[v]) - speed_below * (cell[v] - below[v]))
        for v in range(5)
    ]


def pack_kernel(slot_hbm, near_hbm, state_hbm, out_ref, pick_ref, slot_ref, near_ref, state_ref, sems):
    copies = [
        pltpu.make_async_copy(source, target, sems.at[i])
        for i, (source, target) in enumerate(
            (
                (state_hbm.at[0], state_ref.at[0]),
                (state_hbm.at[1], state_ref.at[1]),
                (slot_hbm, slot_ref),
                (near_hbm, near_ref),
            )
        )
    ]
    for copy in copies:
        copy.start()
    count = out_ref.shape[0] // SLOT
    boxes = 2 * count
    best = None
    for box in range(2):
        copies[box].wait()
        cell = [state_ref[box, v] for v in range(5)]
        for v in range(5):
            for half in range(2):
                row = ROWS * box + 2 * v + half
                out_ref[pl.ds(row, count, stride=SLOT), :] = cell[v][:, LANES * half : LANES * (half + 1)]
        velocity, _, sound = primitives(cell)
        largest = jnp.maximum(jnp.maximum(jnp.abs(velocity[0]), jnp.abs(velocity[1])), jnp.abs(velocity[2]))
        speed = largest + sound
        best = speed if best is None else jnp.maximum(best, speed)
    best = jnp.max(jnp.max(best, axis=0, keepdims=True), axis=1, keepdims=True)

    def place(index):
        local = lax.rem(index, boxes)
        return lax.rem(local, 2) * count + lax.div(local, 2)

    copies[2].wait()
    copies[3].wait()
    values = [place(slot_ref[0]), place(slot_ref[1])]
    for box in range(2):
        values += [place(near_ref[box, 2]), place(near_ref[box, 3])]
    lane = lane_index((count, LANES))
    header = jnp.where(lane == 6, jnp.broadcast_to(best, lane.shape), 0.0)
    for position, value in enumerate(values):
        header = jnp.where(lane == position, value.astype(jnp.float32), header)
    out_ref[pl.ds(20, count, stride=SLOT), :] = header
    for row in range(21, SLOT):
        out_ref[pl.ds(row, count, stride=SLOT), :] = jnp.zeros((count, LANES), jnp.float32)

    segment = lax.axis_index(SEG)
    lane = lane_index(pick_ref.shape)
    picks = jnp.zeros(pick_ref.shape, jnp.float32)
    for box in range(2):
        for face in (0, 1, 4, 5):
            index = near_ref[box, face]
            value = lax.rem(index, 2)
            if face < 2:
                value = value + jnp.where(lax.div(index, boxes) == segment, 2, 0)
            picks = jnp.where(lane == 6 * box + face, value.astype(jnp.float32), picks)
    pick_ref[...] = picks


def three_parts(value):
    high = value.astype(jnp.bfloat16)
    rest = value - high.astype(jnp.float32)
    middle = rest.astype(jnp.bfloat16)
    low = (rest - middle.astype(jnp.float32)).astype(jnp.bfloat16)
    return jnp.concatenate([high, middle, low], axis=0)


def gather_rows(one_hot, parts):
    chosen = jnp.where(one_hot, 1.0, 0.0).astype(jnp.bfloat16)
    return jnp.dot(jnp.concatenate([chosen] * 3, axis=1), parts, preferred_element_type=jnp.float32)


def route_kernel(in_ref, out_ref, best_ref):
    count = in_ref.shape[0] // SLOT
    boxes = 2 * count
    header = in_ref[pl.ds(20, count, stride=SLOT), :]
    best = jnp.max(jnp.where(lane_index(header.shape) == 6, header, 0.0), axis=0, keepdims=True)
    best = jnp.max(best, axis=1, keepdims=True)
    best_ref[...] = jnp.broadcast_to(best.reshape(1, 1, 1), best_ref.shape)
    both = jnp.concatenate([header, pltpu.roll(header, LANES - 1, 1)], axis=0)
    target = jnp.broadcast_to(jnp.transpose(both)[0:1, :], (boxes, boxes))
    index = lax.broadcasted_iota(jnp.int32, (boxes, boxes), 0).astype(jnp.float32)

    def beside(first, second):
        rows = jnp.concatenate([header[:, first : first + 1], header[:, second : second + 1]], axis=0)
        return jnp.broadcast_to(rows, (boxes, boxes))

    columns = []
    for row in range(ROWS):
        columns.append(
            jnp.concatenate(
                [in_ref[pl.ds(ROWS * box + row, count, stride=SLOT), :] for box in range(2)], axis=0
            )
        )
    lane2 = lane_index((boxes, LANES))
    last = jnp.zeros((boxes, LANES), jnp.float32)
    first = jnp.zeros((boxes, LANES), jnp.float32)
    for v in range(5):
        mine = (lane2 >= 16 * v) & (lane2 < 16 * (v + 1))
        last = jnp.where(mine, pltpu.roll(columns[2 * v + 1], 16 * (v + 1), 1), last)
        first = jnp.where(mine, pltpu.roll(columns[2 * v], 16 * v, 1) if v else columns[0], first)
    placed = gather_rows(index == target, three_parts(jnp.concatenate(columns, axis=1)))
    below = gather_rows(beside(2, 4) == target, three_parts(last))
    above = gather_rows(beside(3, 5) == target, three_parts(first))
    for box in range(2):
        rows = slice(count * box, count * (box + 1))
        for row in range(ROWS):
            out_ref[pl.ds(ROWS * box + row, count, stride=SLOT), :] = placed[rows, LANES * row : LANES * (row + 1)]
        out_ref[pl.ds(20 + box, count, stride=SLOT), :] = below[rows]
        out_ref[pl.ds(22 + box, count, stride=SLOT), :] = above[rows]


def peak_kernel(in_ref, out_ref):
    best = jnp.max(in_ref[...], axis=0, keepdims=True)
    out_ref[...] = jnp.broadcast_to(best, out_ref.shape)


def change_kernel(pick_ref, in_ref, before_ref, after_ref, out_ref):
    count = in_ref.shape[0] // SLOT

    def rows_of(row):
        return in_ref[pl.ds(row, count, stride=SLOT), :]

    def pick(box, face):
        return pick_ref[0:1, 6 * box + face : 6 * box + face + 1]

    cell = [
        jnp.stack([rows_of(ROWS * box + 2 * v + half) for box in range(2) for half in range(2)]) for v in range(5)
    ]
    velocity, _, sound = primitives(cell)
    lane = lane_index(cell[0].shape)

    own = (in_ref[SLOT * (count - 1) : SLOT * count, :], in_ref[0:SLOT, :])
    other = (before_ref[...], after_ref[...])
    ghosts = []
    for face in range(2):
        for box in range(2):
            wanted = pick(box, face)
            rows = jnp.where(wanted >= 2.0, own[face], other[face])
            first = (wanted == 0.0) | (wanted == 2.0)
            ghosts.append(jnp.where(first, rows[0:ROWS], rows[ROWS : 2 * ROWS]))
    layer = lax.broadcasted_iota(jnp.int32, cell[0].shape, 1)
    below, above = [], []
    for v in range(5):

        def spread(rows):
            return jnp.stack([rows[box][2 * v + half : 2 * v + half + 1] for box in range(2) for half in range(2)])

        below.append(jnp.where(layer == 0, spread(ghosts[0:2]), pltpu.roll(cell[v], 1, 1)))
        above.append(jnp.where(layer == count - 1, spread(ghosts[2:4]), pltpu.roll(cell[v], count - 1, 1)))
    change = axis_change(cell, jnp.abs(velocity[0]) + sound, below, above, 0)

    ghost_low = [rows_of(20 + box) for box in range(2)]
    ghost_high = [rows_of(22 + box) for box in range(2)]
    below, above = [], []
    for v in range(5):
        low = [pltpu.roll(g, LANES - 16 * v, 1) if v else g for g in ghost_low]
        high = [pltpu.roll(g, 112 - 16 * v, 1) for g in ghost_high]
        rolled = pltpu.roll(cell[v], 16, 2)
        edge = jnp.stack([low[0], rolled[0], low[1], rolled[2]])
        below.append(jnp.where(lane < 16, edge, rolled))
        rolled = pltpu.roll(cell[v], LANES - 16, 2)
        edge = jnp.stack([rolled[1], high[0], rolled[3], high[1]])
        above.append(jnp.where(lane >= LANES - 16, edge, rolled))
    more = axis_change(cell, jnp.abs(velocity[1]) + sound, below, above, 1)
    change = [change[v] + more[v] for v in range(5)]

    deep = lane & 15
    below, above = [], []
    slots = [[pick(box, face) == 0.0 for box in range(2)] for face in (4, 5)]
    for v in range(5):
        wrapped = pltpu.roll(cell[v], LANES - 15, 2)
        edge = jnp.concatenate([jnp.where(slots[0][box], wrapped[0:2], wrapped[2:4]) for box in range(2)], axis=0)
        below.append(jnp.where(deep == 0, edge, pltpu.roll(cell[v], 1, 2)))
        wrapped = pltpu.roll(cell[v], 15, 2)
        edge = jnp.concatenate([jnp.where(slots[1][box], wrapped[0:2], wrapped[2:4]) for box in range(2)], axis=0)
        above.append(jnp.where(deep == 15, edge, pltpu.roll(cell[v], LANES - 1, 2)))
    more = axis_change(cell, jnp.abs(velocity[2]) + sound, below, above, 2)

    for v in range(5):
        out_ref[v] = change[v] + more[v]


def finish_kernel(in_ref, change_ref, best_ref, out_ref):
    count = in_ref.shape[0] // SLOT
    step = courant / jnp.max(best_ref[...], axis=0)
    for box in range(2):
        for v in range(5):
            for half in range(2):
                cell = in_ref[pl.ds(ROWS * box + 2 * v + half, count, stride=SLOT), :]
                columns = slice(LANES * half, LANES * (half + 1))
                out_ref[box, v, :, columns] = cell - step * change_ref[v, 2 * box + half]


def local(state, new_slot, neighbours):
    count = lax.axis_size("curve")
    along_x, along_z = (lax.axis_size(axis) for axis in SEG)
    segs = along_x * along_z
    f32 = jnp.float32
    sent, pick = pl.pallas_call(
        pack_kernel,
        out_shape=(jax.ShapeDtypeStruct((SLOT * count, LANES), f32), jax.ShapeDtypeStruct((8, LANES), f32)),
        in_specs=[hbm, hbm, hbm],
        out_specs=(vmem, vmem),
        scratch_shapes=[
            pltpu.SMEM(new_slot.shape, jnp.int32),
            pltpu.SMEM(neighbours.shape, jnp.int32),
            pltpu.VMEM(state.shape, f32),
            pltpu.SemaphoreType.DMA((4,)),
        ],
        name="pack",
    )(new_slot, neighbours, state)
    met = lax.all_to_all(sent.reshape(count, SLOT, LANES), "curve", 0, 0, tiled=True)
    routed, best = pl.pallas_call(
        route_kernel,
        out_shape=(
            jax.ShapeDtypeStruct((SLOT * count, LANES), f32),
            jax.ShapeDtypeStruct((along_x, 1, LANES), f32),
        ),
        in_specs=[vmem],
        out_specs=(vmem, vmem),
        compiler_params=params,
        name="route",
    )(met.reshape(SLOT * count, LANES))
    moved = lax.all_to_all(routed.reshape(count, SLOT, LANES), "curve", 0, 0, tiled=True)
    up = [(i, (i + 1) % segs) for i in range(segs)]
    down = [(j, i) for i, j in up]
    best = lax.all_to_all(best, SEG[0], 0, 0, tiled=True)
    before = lax.ppermute(moved[count - 1], SEG, up)
    after = lax.ppermute(moved[0], SEG, down)
    best = pl.pallas_call(
        peak_kernel,
        out_shape=jax.ShapeDtypeStruct((along_z, 1, LANES), f32),
        in_specs=[vmem],
        out_specs=vmem,
        compiler_params=params,
        name="peak",
    )(best)
    best = lax.all_to_all(best, SEG[1], 0, 0, tiled=True)
    moved = moved.reshape(SLOT * count, LANES)
    change = pl.pallas_call(
        change_kernel,
        out_shape=jax.ShapeDtypeStruct((5, 4, count, LANES), f32),
        in_specs=[vmem] * 4,
        out_specs=vmem,
        compiler_params=params,
        name="change",
    )(pick, moved, before, after)
    return pl.pallas_call(
        finish_kernel,
        out_shape=jax.ShapeDtypeStruct(state.shape, f32),
        in_specs=[vmem] * 3,
        out_specs=vmem,
        compiler_params=params,
        name="finish",
    )(moved, change, best)


def solution(mesh):
    segs, count = mesh.devices.shape
    side_x = math.isqrt(segs)
    grid = Mesh(mesh.devices.reshape(side_x, segs // side_x, count), SEG + ("curve",))
    placed = P(SEG + ("curve",))
    return jax.shard_map(
        local, mesh=grid, in_specs=(placed, placed, placed), out_specs=placed, check_vma=False
    )
```

```python
import jax
import jax.numpy as jnp
from jax import lax
from jax.experimental import pallas as pl
from jax.experimental.pallas import tpu as pltpu
from jax.sharding import PartitionSpec as P

gamma_ratio = 1.4
courant = 0.3

LANES = 128
ROWS = 10
SLOT = 24
WIDE = 48

vmem = pl.BlockSpec(memory_space=pltpu.VMEM)
hbm = pl.BlockSpec(memory_space=pltpu.HBM)
params = pltpu.CompilerParams(vmem_limit_bytes=16 * 2**20)


def lane_index(shape):
    return lax.broadcasted_iota(jnp.int32, shape, len(shape) - 1)


def primitives(cell):
    inverse = 1.0 / cell[0]
    velocity = [cell[1 + d] * inverse for d in range(3)]
    kinetic = 0.5 * (cell[1] * velocity[0] + cell[2] * velocity[1] + cell[3] * velocity[2])
    pressure = (gamma_ratio - 1.0) * (cell[4] - kinetic)
    sound = jnp.sqrt(gamma_ratio * pressure * inverse)
    return velocity, pressure, sound


def side(cell, axis_num):
    velocity, pressure, sound = primitives(cell)
    along = velocity[axis_num]
    flux = [cell[1 + axis_num]]
    for d in range(3):
        term = cell[1 + d] * along
        flux.append(term + pressure if d == axis_num else term)
    flux.append((cell[4] + pressure) * along)
    return flux, jnp.abs(along) + sound


def axis_change(cell, speed, below, above, axis_num):
    flux_below, speed_below = side(below, axis_num)
    flux_above, speed_above = side(above, axis_num)
    speed_below = jnp.maximum(speed, speed_below)
    speed_above = jnp.maximum(speed, speed_above)
    return [
        0.5 * (flux_above[v] - flux_below[v])
        - 0.5 * (speed_above * (above[v] - cell[v]) - speed_below * (cell[v] - below[v]))
        for v in range(5)
    ]


def pack_kernel(
    slot_hbm, near_hbm, state_hbm, out_ref, first_ref, last_ref, pick_ref, slot_ref, near_ref, state_ref, sems
):
    copies = [
        pltpu.make_async_copy(source, target, sems.at[i])
        for i, (source, target) in enumerate(
            (
                (state_hbm.at[0], state_ref.at[0]),
                (state_hbm.at[1], state_ref.at[1]),
                (slot_hbm, slot_ref),
                (near_hbm, near_ref),
            )
        )
    ]
    for copy in copies:
        copy.start()
    count = out_ref.shape[0] // SLOT
    boxes = 2 * count
    best = None
    for box in range(2):
        copies[box].wait()
        cell = [state_ref[box, v] for v in range(5)]
        for v in range(5):
            for half in range(2):
                row = ROWS * box + 2 * v + half
                part = cell[v][:, LANES * half : LANES * (half + 1)]
                out_ref[pl.ds(row, count, stride=SLOT), :] = part
                first_ref[row : row + 1, :] = part[0:1]
                last_ref[row : row + 1, :] = part[count - 1 : count]
        velocity, _, sound = primitives(cell)
        largest = jnp.maximum(jnp.maximum(jnp.abs(velocity[0]), jnp.abs(velocity[1])), jnp.abs(velocity[2]))
        speed = largest + sound
        best = speed if best is None else jnp.maximum(best, speed)
    best = jnp.max(jnp.max(best, axis=0, keepdims=True), axis=1, keepdims=True)

    def place(index):
        local = lax.rem(index, boxes)
        return lax.rem(local, 2) * count + lax.div(local, 2)

    copies[2].wait()
    copies[3].wait()
    values = [place(slot_ref[0]), place(slot_ref[1])]
    for box in range(2):
        values += [place(near_ref[box, 2]), place(near_ref[box, 3])]
    lane = lane_index((count, LANES))
    header = jnp.where(lane == 6, jnp.broadcast_to(best, lane.shape), 0.0)
    for position, value in enumerate(values):
        header = jnp.where(lane == position, value.astype(jnp.float32), header)
    out_ref[pl.ds(20, count, stride=SLOT), :] = header
    first_ref[2 * ROWS : SLOT, :] = header[0 : SLOT - 2 * ROWS]
    last_ref[2 * ROWS : SLOT, :] = header[0 : SLOT - 2 * ROWS]
    for row in range(21, SLOT):
        out_ref[pl.ds(row, count, stride=SLOT), :] = jnp.zeros((count, LANES), jnp.float32)

    segment = lax.axis_index("seg")
    lane = lane_index(pick_ref.shape)
    picks = jnp.zeros(pick_ref.shape, jnp.float32)
    for box in range(2):
        for face in (0, 1, 4, 5):
            index = near_ref[box, face]
            value = lax.rem(index, 2)
            if face < 2:
                value = value + jnp.where(lax.div(index, boxes) == segment, 2, 0)
            picks = jnp.where(lane == 6 * box + face, value.astype(jnp.float32), picks)
    pick_ref[...] = picks


def three_parts(value):
    high = value.astype(jnp.bfloat16)
    rest = value - high.astype(jnp.float32)
    middle = rest.astype(jnp.bfloat16)
    low = (rest - middle.astype(jnp.float32)).astype(jnp.bfloat16)
    return jnp.concatenate([high, middle, low], axis=0)


def gather_rows(one_hot, parts):
    chosen = jnp.where(one_hot, 1.0, 0.0).astype(jnp.bfloat16)
    return jnp.dot(jnp.concatenate([chosen] * 3, axis=1), parts, preferred_element_type=jnp.float32)


def route_kernel(in_ref, before_ref, after_ref, out_ref, best_ref):
    count = in_ref.shape[0] // SLOT
    boxes = 2 * count
    header = in_ref[pl.ds(20, count, stride=SLOT), :]
    lane = lane_index((count, LANES))
    best = jnp.max(jnp.where(lane == 6, header, 0.0), axis=0, keepdims=True)
    best = jnp.max(best, axis=1, keepdims=True)
    best_ref[...] = jnp.broadcast_to(best.reshape(1, 1, 1), best_ref.shape)
    both = jnp.concatenate([header, pltpu.roll(header, LANES - 1, 1)], axis=0)
    target = jnp.broadcast_to(jnp.transpose(both)[0:1, :], (boxes, boxes))
    index = lax.broadcasted_iota(jnp.int32, (boxes, boxes), 0).astype(jnp.float32)

    def beside(first, second):
        rows = jnp.concatenate([header[:, first : first + 1], header[:, second : second + 1]], axis=0)
        return jnp.broadcast_to(rows, (boxes, boxes))

    columns = []
    for row in range(ROWS):
        columns.append(
            jnp.concatenate(
                [in_ref[pl.ds(ROWS * box + row, count, stride=SLOT), :] for box in range(2)], axis=0
            )
        )
    lane2 = lane_index((boxes, LANES))
    last = jnp.zeros((boxes, LANES), jnp.float32)
    first = jnp.zeros((boxes, LANES), jnp.float32)
    for v in range(5):
        mine = (lane2 >= 16 * v) & (lane2 < 16 * (v + 1))
        last = jnp.where(mine, pltpu.roll(columns[2 * v + 1], 16 * (v + 1), 1), last)
        first = jnp.where(mine, pltpu.roll(columns[2 * v], 16 * v, 1) if v else columns[0], first)
    placed = gather_rows(index == target, three_parts(jnp.concatenate(columns, axis=1)))
    below = gather_rows(beside(2, 4) == target, three_parts(last))
    above = gather_rows(beside(3, 5) == target, three_parts(first))
    for box in range(2):
        rows = slice(count * box, count * (box + 1))
        for row in range(ROWS):
            out_ref[pl.ds(ROWS * box + row, count, stride=WIDE), :] = placed[rows, LANES * row : LANES * (row + 1)]
        out_ref[pl.ds(20 + box, count, stride=WIDE), :] = below[rows]
        out_ref[pl.ds(22 + box, count, stride=WIDE), :] = above[rows]

    place = lax.broadcasted_iota(jnp.int32, (count, LANES), 0).astype(jnp.float32)
    marks = jnp.zeros((count, LANES), jnp.float32)
    for side_num, face_ref in enumerate((after_ref, before_ref)):
        face = face_ref[...]
        target = [jnp.broadcast_to(face[20:21, box : box + 1], place.shape) for box in range(2)]
        slot = [jnp.where(t >= count, 1.0, 0.0) for t in target]
        here = [place == target[box] - count * slot[box] for box in range(2)]
        for row in range(ROWS):
            value = jnp.where(here[0], face[row : row + 1], face[ROWS + row : ROWS + row + 1])
            out_ref[pl.ds(24 + ROWS * side_num + row, count, stride=WIDE), :] = value
        mark = jnp.where(here[0], slot[0], jnp.where(here[1], slot[1], -1.0))
        marks = jnp.where(lane == side_num, mark, marks)
    for row in range(44, WIDE):
        out_ref[pl.ds(row, count, stride=WIDE), :] = marks


def change_kernel(pick_ref, in_ref, out_ref):
    count = in_ref.shape[0] // WIDE

    def rows_of(row):
        return in_ref[pl.ds(row, count, stride=WIDE), :]

    def pick(box, face):
        return pick_ref[0:1, 6 * box + face : 6 * box + face + 1]

    cell = [
        jnp.stack([rows_of(ROWS * box + 2 * v + half) for box in range(2) for half in range(2)]) for v in range(5)
    ]
    velocity, _, sound = primitives(cell)
    lane = lane_index(cell[0].shape)

    marks = rows_of(44)
    own = (in_ref[WIDE * (count - 1) : WIDE * (count - 1) + SLOT, :], in_ref[0:SLOT, :])
    ghosts = []
    for face in range(2):
        start = 34 - ROWS * face
        mark = jnp.broadcast_to(marks[:, 1 - face : 2 - face], (count, LANES))
        strips = [rows_of(start + row) for row in range(ROWS)]
        for box in range(2):
            wanted = pick(box, face)
            mine = mark == wanted
            far = [jnp.sum(jnp.where(mine, strip, 0.0), axis=0, keepdims=True) for strip in strips]
            near = jnp.where(wanted == 2.0, own[face][0:ROWS], own[face][ROWS : 2 * ROWS])
            inside = wanted >= 2.0
            ghosts.append([jnp.where(inside, near[row : row + 1], far[row]) for row in range(ROWS)])
    layer = lax.broadcasted_iota(jnp.int32, cell[0].shape, 1)
    below, above = [], []
    for v in range(5):

        def spread(rows):
            return jnp.stack([rows[box][2 * v + half] for box in range(2) for half in range(2)])

        below.append(jnp.where(layer == 0, spread(ghosts[0:2]), pltpu.roll(cell[v], 1, 1)))
        above.append(jnp.where(layer == count - 1, spread(ghosts[2:4]), pltpu.roll(cell[v], count - 1, 1)))
    change = axis_change(cell, jnp.abs(velocity[0]) + sound, below, above, 0)

    ghost_low = [rows_of(20 + box) for box in range(2)]
    ghost_high = [rows_of(22 + box) for box in range(2)]
    below, above = [], []
    for v in range(5):
        low = [pltpu.roll(g, LANES - 16 * v, 1) if v else g for g in ghost_low]
        high = [pltpu.roll(g, 112 - 16 * v, 1) for g in ghost_high]
        rolled = pltpu.roll(cell[v], 16, 2)
        edge = jnp.stack([low[0], rolled[0], low[1], rolled[2]])
        below.append(jnp.where(lane < 16, edge, rolled))
        rolled = pltpu.roll(cell[v], LANES - 16, 2)
        edge = jnp.stack([rolled[1], high[0], rolled[3], high[1]])
        above.append(jnp.where(lane >= LANES - 16, edge, rolled))
    more = axis_change(cell, jnp.abs(velocity[1]) + sound, below, above, 1)
    change = [change[v] + more[v] for v in range(5)]

    deep = lane & 15
    below, above = [], []
    slots = [[pick(box, face) == 0.0 for box in range(2)] for face in (4, 5)]
    for v in range(5):
        wrapped = pltpu.roll(cell[v], LANES - 15, 2)
        edge = jnp.concatenate([jnp.where(slots[0][box], wrapped[0:2], wrapped[2:4]) for box in range(2)], axis=0)
        below.append(jnp.where(deep == 0, edge, pltpu.roll(cell[v], 1, 2)))
        wrapped = pltpu.roll(cell[v], 15, 2)
        edge = jnp.concatenate([jnp.where(slots[1][box], wrapped[0:2], wrapped[2:4]) for box in range(2)], axis=0)
        above.append(jnp.where(deep == 15, edge, pltpu.roll(cell[v], LANES - 1, 2)))
    more = axis_change(cell, jnp.abs(velocity[2]) + sound, below, above, 2)

    for v in range(5):
        out_ref[v] = change[v] + more[v]


def finish_kernel(in_ref, change_ref, best_ref, out_ref):
    count = in_ref.shape[0] // WIDE
    step = courant / jnp.max(best_ref[...], axis=0)
    for box in range(2):
        for v in range(5):
            for half in range(2):
                cell = in_ref[pl.ds(ROWS * box + 2 * v + half, count, stride=WIDE), :]
                columns = slice(LANES * half, LANES * (half + 1))
                out_ref[box, v, :, columns] = cell - step * change_ref[v, 2 * box + half]


def local(state, new_slot, neighbours):
    count = lax.axis_size("curve")
    segs = lax.axis_size("seg")
    f32 = jnp.float32
    sent, first, last, pick = pl.pallas_call(
        pack_kernel,
        out_shape=(
            jax.ShapeDtypeStruct((SLOT * count, LANES), f32),
            jax.ShapeDtypeStruct((SLOT, LANES), f32),
            jax.ShapeDtypeStruct((SLOT, LANES), f32),
            jax.ShapeDtypeStruct((8, LANES), f32),
        ),
        in_specs=[hbm, hbm, hbm],
        out_specs=(vmem, vmem, vmem, vmem),
        scratch_shapes=[
            pltpu.SMEM(new_slot.shape, jnp.int32),
            pltpu.SMEM(neighbours.shape, jnp.int32),
            pltpu.VMEM(state.shape, f32),
            pltpu.SemaphoreType.DMA((4,)),
        ],
        name="pack",
    )(new_slot, neighbours, state)
    up = [(i, (i + 1) % segs) for i in range(segs)]
    down = [(j, i) for i, j in up]
    met = lax.all_to_all(sent.reshape(count, SLOT, LANES), "curve", 0, 0, tiled=True)
    before = lax.ppermute(last, "seg", up)
    after = lax.ppermute(first, "seg", down)
    routed, best = pl.pallas_call(
        route_kernel,
        out_shape=(
            jax.ShapeDtypeStruct((WIDE * count, LANES), f32),
            jax.ShapeDtypeStruct((segs, 1, LANES), f32),
        ),
        in_specs=[vmem, vmem, vmem],
        out_specs=(vmem, vmem),
        compiler_params=params,
        name="route",
    )(met.reshape(SLOT * count, LANES), before, after)
    moved = lax.all_to_all(routed.reshape(count, WIDE, LANES), "curve", 0, 0, tiled=True)
    moved, best = lax.optimization_barrier((moved, best))
    best = lax.all_to_all(best, "seg", 0, 0, tiled=True)
    moved = moved.reshape(WIDE * count, LANES)
    change = pl.pallas_call(
        change_kernel,
        out_shape=jax.ShapeDtypeStruct((5, 4, count, LANES), f32),
        in_specs=[vmem, vmem],
        out_specs=vmem,
        compiler_params=params,
        name="change",
    )(pick, moved)
    return pl.pallas_call(
        finish_kernel,
        out_shape=jax.ShapeDtypeStruct(state.shape, f32),
        in_specs=[vmem] * 3,
        out_specs=vmem,
        compiler_params=params,
        name="finish",
    )(moved, change, best)


def solution(mesh):
    placed = P(("seg", "curve"))
    return jax.shard_map(
        local, mesh=mesh, in_specs=(placed, placed, placed), out_specs=placed, check_vma=False
    )
```

```python
import math

import jax
import jax.numpy as jnp
from jax import lax
from jax.experimental import pallas as pl
from jax.experimental.pallas import tpu as pltpu
from jax.sharding import Mesh, PartitionSpec as P

gamma_ratio = 1.4
courant = 0.3

LANES = 128
SEG = ("seg_x", "seg_z")
ROWS = 10
SLOT = 24

vmem = pl.BlockSpec(memory_space=pltpu.VMEM)
hbm = pl.BlockSpec(memory_space=pltpu.HBM)
params = pltpu.CompilerParams(vmem_limit_bytes=16 * 2**20)


def lane_index(shape):
    return lax.broadcasted_iota(jnp.int32, shape, len(shape) - 1)


def primitives(cell):
    inverse = 1.0 / cell[0]
    velocity = [cell[1 + d] * inverse for d in range(3)]
    kinetic = 0.5 * (cell[1] * velocity[0] + cell[2] * velocity[1] + cell[3] * velocity[2])
    pressure = (gamma_ratio - 1.0) * (cell[4] - kinetic)
    sound = jnp.sqrt(gamma_ratio * pressure * inverse)
    return velocity, pressure, sound


def side(cell, axis_num):
    velocity, pressure, sound = primitives(cell)
    along = velocity[axis_num]
    flux = [cell[1 + axis_num]]
    for d in range(3):
        term = cell[1 + d] * along
        flux.append(term + pressure if d == axis_num else term)
    flux.append((cell[4] + pressure) * along)
    return flux, jnp.abs(along) + sound


def axis_change(cell, speed, below, above, axis_num):
    flux_below, speed_below = side(below, axis_num)
    flux_above, speed_above = side(above, axis_num)
    speed_below = jnp.maximum(speed, speed_below)
    speed_above = jnp.maximum(speed, speed_above)
    return [
        0.5 * (flux_above[v] - flux_below[v])
        - 0.5 * (speed_above * (above[v] - cell[v]) - speed_below * (cell[v] - below[v]))
        for v in range(5)
    ]


def pack_kernel(slot_hbm, near_hbm, state_hbm, out_ref, pick_ref, slot_ref, near_ref, state_ref, sems):
    copies = [
        pltpu.make_async_copy(source, target, sems.at[i])
        for i, (source, target) in enumerate(
            (
                (state_hbm.at[0], state_ref.at[0]),
                (state_hbm.at[1], state_ref.at[1]),
                (slot_hbm, slot_ref),
                (near_hbm, near_ref),
            )
        )
    ]
    for copy in copies:
        copy.start()
    count = out_ref.shape[0] // SLOT
    boxes = 2 * count
    best = None
    for box in range(2):
        copies[box].wait()
        cell = [state_ref[box, v] for v in range(5)]
        for v in range(5):
            for half in range(2):
                row = ROWS * box + 2 * v + half
                out_ref[pl.ds(row, count, stride=SLOT), :] = cell[v][:, LANES * half : LANES * (half + 1)]
        velocity, _, sound = primitives(cell)
        largest = jnp.maximum(jnp.maximum(jnp.abs(velocity[0]), jnp.abs(velocity[1])), jnp.abs(velocity[2]))
        speed = largest + sound
        best = speed if best is None else jnp.maximum(best, speed)
    best = jnp.max(jnp.max(best, axis=0, keepdims=True), axis=1, keepdims=True)

    def place(index):
        local = lax.rem(index, boxes)
        return lax.rem(local, 2) * count + lax.div(local, 2)

    copies[2].wait()
    copies[3].wait()
    values = [place(slot_ref[0]), place(slot_ref[1])]
    for box in range(2):
        values += [place(near_ref[box, 2]), place(near_ref[box, 3])]
    lane = lane_index((count, LANES))
    header = jnp.where(lane == 6, jnp.broadcast_to(best, lane.shape), 0.0)
    for position, value in enumerate(values):
        header = jnp.where(lane == position, value.astype(jnp.float32), header)
    out_ref[pl.ds(20, count, stride=SLOT), :] = header
    for row in range(21, SLOT):
        out_ref[pl.ds(row, count, stride=SLOT), :] = jnp.zeros((count, LANES), jnp.float32)

    segment = lax.axis_index(SEG)
    lane = lane_index(pick_ref.shape)
    picks = jnp.zeros(pick_ref.shape, jnp.float32)
    for box in range(2):
        for face in (0, 1, 4, 5):
            index = near_ref[box, face]
            value = lax.rem(index, 2)
            if face < 2:
                value = value + jnp.where(lax.div(index, boxes) == segment, 2, 0)
            picks = jnp.where(lane == 6 * box + face, value.astype(jnp.float32), picks)
    pick_ref[...] = picks


def three_parts(value):
    high = value.astype(jnp.bfloat16)
    rest = value - high.astype(jnp.float32)
    middle = rest.astype(jnp.bfloat16)
    low = (rest - middle.astype(jnp.float32)).astype(jnp.bfloat16)
    return jnp.concatenate([high, middle, low], axis=0)


def gather_rows(one_hot, parts):
    chosen = jnp.where(one_hot, 1.0, 0.0).astype(jnp.bfloat16)
    return jnp.dot(jnp.concatenate([chosen] * 3, axis=1), parts, preferred_element_type=jnp.float32)


def route_kernel(in_ref, out_ref, best_ref):
    count = in_ref.shape[0] // SLOT
    boxes = 2 * count
    header = in_ref[pl.ds(20, count, stride=SLOT), :]
    best = jnp.max(jnp.where(lane_index(header.shape) == 6, header, 0.0), axis=0, keepdims=True)
    best = jnp.max(best, axis=1, keepdims=True)
    best_ref[...] = jnp.broadcast_to(best, best_ref.shape)
    both = jnp.concatenate([header, pltpu.roll(header, LANES - 1, 1)], axis=0)
    target = jnp.broadcast_to(jnp.transpose(both)[0:1, :], (boxes, boxes))
    index = lax.broadcasted_iota(jnp.int32, (boxes, boxes), 0).astype(jnp.float32)

    def beside(first, second):
        rows = jnp.concatenate([header[:, first : first + 1], header[:, second : second + 1]], axis=0)
        return jnp.broadcast_to(rows, (boxes, boxes))

    columns = []
    for row in range(ROWS):
        columns.append(
            jnp.concatenate(
                [in_ref[pl.ds(ROWS * box + row, count, stride=SLOT), :] for box in range(2)], axis=0
            )
        )
    lane2 = lane_index((boxes, LANES))
    last = jnp.zeros((boxes, LANES), jnp.float32)
    first = jnp.zeros((boxes, LANES), jnp.float32)
    for v in range(5):
        mine = (lane2 >= 16 * v) & (lane2 < 16 * (v + 1))
        last = jnp.where(mine, pltpu.roll(columns[2 * v + 1], 16 * (v + 1), 1), last)
        first = jnp.where(mine, pltpu.roll(columns[2 * v], 16 * v, 1) if v else columns[0], first)
    placed = gather_rows(index == target, three_parts(jnp.concatenate(columns, axis=1)))
    below = gather_rows(beside(2, 4) == target, three_parts(last))
    above = gather_rows(beside(3, 5) == target, three_parts(first))
    for box in range(2):
        rows = slice(count * box, count * (box + 1))
        for row in range(ROWS):
            out_ref[pl.ds(ROWS * box + row, count, stride=SLOT), :] = placed[rows, LANES * row : LANES * (row + 1)]
        out_ref[pl.ds(20 + box, count, stride=SLOT), :] = below[rows]
        out_ref[pl.ds(22 + box, count, stride=SLOT), :] = above[rows]


def rows_of(ref, row):
    return ref[pl.ds(row, ref.shape[0] // SLOT, stride=SLOT), :]


def load_cells(ref):
    return [
        jnp.stack([rows_of(ref, ROWS * box + 2 * v + half) for box in range(2) for half in range(2)])
        for v in range(5)
    ]


def pick(ref, box, face):
    return ref[0:1, 6 * box + face : 6 * box + face + 1]


def edge_layers(ref):
    end = ref.shape[0]
    return ref[0:SLOT, :], ref[end - SLOT : end, :]


def with_speed(rows, speed):
    return jnp.where(lax.broadcasted_iota(jnp.int32, rows.shape, 0) < 2 * ROWS, rows, speed)


def slot_of(ref, place, step):
    count = ref.shape[0] // SLOT
    index = lax.rem(place + step + count, count)
    return ref[pl.ds(pl.multiple_of(index * SLOT, SLOT), SLOT), :]


def fill_slots(ref, place, to_next, to_previous):
    count = ref.shape[0] // SLOT
    following = lax.rem(place + 1, count)
    for slot in range(count):
        ref[SLOT * slot : SLOT * (slot + 1), :] = jnp.where(following == slot, to_next, to_previous)


def along_x_kernel(in_ref, best_ref, out_ref):
    first, last = edge_layers(in_ref)
    best = best_ref[0:1, :]
    fill_slots(out_ref, lax.axis_index(SEG[0]), with_speed(last, best), with_speed(first, best))


def along_z_kernel(in_ref, met_ref, out_ref):
    first, last = edge_layers(in_ref)
    best = jnp.max(rows_of(met_ref, 2 * ROWS), axis=0, keepdims=True)
    place_x, place_z = (lax.axis_index(axis) for axis in SEG)
    end = out_ref.shape[0] // SLOT - 1
    last = jnp.where(place_z == end, slot_of(met_ref, place_x, -1), last)
    first = jnp.where(place_z == 0, slot_of(met_ref, place_x, 1), first)
    fill_slots(out_ref, place_z, with_speed(last, best), with_speed(first, best))


def planes_kernel(pick_ref, in_ref, out_ref):
    cell = load_cells(in_ref)
    velocity, _, sound = primitives(cell)
    lane = lane_index(cell[0].shape)

    ghost_low = [rows_of(in_ref, 20 + box) for box in range(2)]
    ghost_high = [rows_of(in_ref, 22 + box) for box in range(2)]
    below, above = [], []
    for v in range(5):
        low = [pltpu.roll(g, LANES - 16 * v, 1) if v else g for g in ghost_low]
        high = [pltpu.roll(g, 112 - 16 * v, 1) for g in ghost_high]
        rolled = pltpu.roll(cell[v], 16, 2)
        edge = jnp.stack([low[0], rolled[0], low[1], rolled[2]])
        below.append(jnp.where(lane < 16, edge, rolled))
        rolled = pltpu.roll(cell[v], LANES - 16, 2)
        edge = jnp.stack([rolled[1], high[0], rolled[3], high[1]])
        above.append(jnp.where(lane >= LANES - 16, edge, rolled))
    change = axis_change(cell, jnp.abs(velocity[1]) + sound, below, above, 1)

    deep = lane & 15
    below, above = [], []
    slots = [[pick(pick_ref, box, face) == 0.0 for box in range(2)] for face in (4, 5)]
    for v in range(5):
        wrapped = pltpu.roll(cell[v], LANES - 15, 2)
        edge = jnp.concatenate([jnp.where(slots[0][box], wrapped[0:2], wrapped[2:4]) for box in range(2)], axis=0)
        below.append(jnp.where(deep == 0, edge, pltpu.roll(cell[v], 1, 2)))
        wrapped = pltpu.roll(cell[v], 15, 2)
        edge = jnp.concatenate([jnp.where(slots[1][box], wrapped[0:2], wrapped[2:4]) for box in range(2)], axis=0)
        above.append(jnp.where(deep == 15, edge, pltpu.roll(cell[v], LANES - 1, 2)))
    more = axis_change(cell, jnp.abs(velocity[2]) + sound, below, above, 2)

    for v in range(5):
        out_ref[v] = change[v] + more[v]


def finish_kernel(pick_ref, in_ref, change_ref, met_ref, out_ref):
    count = in_ref.shape[0] // SLOT
    cell = load_cells(in_ref)
    velocity, _, sound = primitives(cell)
    own = (in_ref[SLOT * (count - 1) : SLOT * count, :], in_ref[0:SLOT, :])
    place = lax.axis_index(SEG[1])
    other = (slot_of(met_ref, place, -1), slot_of(met_ref, place, 1))
    ghosts = []
    for face in range(2):
        for box in range(2):
            wanted = pick(pick_ref, box, face)
            rows = jnp.where(wanted >= 2.0, own[face], other[face])
            first = (wanted == 0.0) | (wanted == 2.0)
            ghosts.append(jnp.where(first, rows[0:ROWS], rows[ROWS : 2 * ROWS]))
    layer = lax.broadcasted_iota(jnp.int32, cell[0].shape, 1)
    below, above = [], []
    for v in range(5):

        def spread(rows):
            return jnp.stack([rows[box][2 * v + half : 2 * v + half + 1] for box in range(2) for half in range(2)])

        below.append(jnp.where(layer == 0, spread(ghosts[0:2]), pltpu.roll(cell[v], 1, 1)))
        above.append(jnp.where(layer == count - 1, spread(ghosts[2:4]), pltpu.roll(cell[v], count - 1, 1)))
    change = axis_change(cell, jnp.abs(velocity[0]) + sound, below, above, 0)

    step = courant / jnp.max(rows_of(met_ref, 2 * ROWS), axis=0, keepdims=True)
    for v in range(5):
        result = cell[v] - step[None] * (change[v] + change_ref[v])
        for box in range(2):
            for half in range(2):
                out_ref[box, v, :, LANES * half : LANES * (half + 1)] = result[2 * box + half]


def local(state, new_slot, neighbours):
    count = lax.axis_size("curve")
    along_x, along_z = (lax.axis_size(axis) for axis in SEG)
    f32 = jnp.float32
    sent, pick = pl.pallas_call(
        pack_kernel,
        out_shape=(jax.ShapeDtypeStruct((SLOT * count, LANES), f32), jax.ShapeDtypeStruct((8, LANES), f32)),
        in_specs=[hbm, hbm, hbm],
        out_specs=(vmem, vmem),
        scratch_shapes=[
            pltpu.SMEM(new_slot.shape, jnp.int32),
            pltpu.SMEM(neighbours.shape, jnp.int32),
            pltpu.VMEM(state.shape, f32),
            pltpu.SemaphoreType.DMA((4,)),
        ],
        name="pack",
    )(new_slot, neighbours, state)
    met = lax.all_to_all(sent.reshape(count, SLOT, LANES), "curve", 0, 0, tiled=True)
    routed, best = pl.pallas_call(
        route_kernel,
        out_shape=(
            jax.ShapeDtypeStruct((SLOT * count, LANES), f32),
            jax.ShapeDtypeStruct((8, LANES), f32),
        ),
        in_specs=[vmem],
        out_specs=(vmem, vmem),
        compiler_params=params,
        name="route",
    )(met.reshape(SLOT * count, LANES))
    moved = lax.all_to_all(routed.reshape(count, SLOT, LANES), "curve", 0, 0, tiled=True)
    moved = moved.reshape(SLOT * count, LANES)
    along = pl.pallas_call(
        along_x_kernel,
        out_shape=jax.ShapeDtypeStruct((SLOT * along_x, LANES), f32),
        in_specs=[vmem] * 2,
        out_specs=vmem,
        compiler_params=params,
        name="along_x",
    )(moved, best)
    along = lax.all_to_all(along.reshape(along_x, SLOT, LANES), SEG[0], 0, 0, tiled=True)
    along = pl.pallas_call(
        along_z_kernel,
        out_shape=jax.ShapeDtypeStruct((SLOT * along_z, LANES), f32),
        in_specs=[vmem] * 2,
        out_specs=vmem,
        compiler_params=params,
        name="along_z",
    )(moved, along.reshape(SLOT * along_x, LANES))
    along = lax.all_to_all(along.reshape(along_z, SLOT, LANES), SEG[1], 0, 0, tiled=True)
    change = pl.pallas_call(
        planes_kernel,
        out_shape=jax.ShapeDtypeStruct((5, 4, count, LANES), f32),
        in_specs=[vmem] * 2,
        out_specs=vmem,
        compiler_params=params,
        name="planes",
    )(pick, moved)
    return pl.pallas_call(
        finish_kernel,
        out_shape=jax.ShapeDtypeStruct(state.shape, f32),
        in_specs=[vmem] * 4,
        out_specs=vmem,
        compiler_params=params,
        name="finish",
    )(pick, moved, change, along.reshape(SLOT * along_z, LANES))


def solution(mesh):
    segs, count = mesh.devices.shape
    side_x = math.isqrt(segs)
    grid = Mesh(mesh.devices.reshape(side_x, segs // side_x, count), SEG + ("curve",))
    placed = P(SEG + ("curve",))
    return jax.shard_map(
        local, mesh=grid, in_specs=(placed, placed, placed), out_specs=placed, check_vma=False
    )
```

```python
import math

import jax
import jax.numpy as jnp
from jax import lax
from jax.experimental import pallas as pl
from jax.experimental.pallas import tpu as pltpu
from jax.sharding import Mesh, PartitionSpec as P

gamma_ratio = 1.4
courant = 0.3

LANES = 128
SEG = ("seg_x", "seg_z")
ROWS = 10
SLOT = 24

vmem = pl.BlockSpec(memory_space=pltpu.VMEM)
hbm = pl.BlockSpec(memory_space=pltpu.HBM)
params = pltpu.CompilerParams(vmem_limit_bytes=16 * 2**20)


def lane_index(shape):
    return lax.broadcasted_iota(jnp.int32, shape, len(shape) - 1)


def primitives(cell):
    inverse = 1.0 / cell[0]
    velocity = [cell[1 + d] * inverse for d in range(3)]
    kinetic = 0.5 * (cell[1] * velocity[0] + cell[2] * velocity[1] + cell[3] * velocity[2])
    pressure = (gamma_ratio - 1.0) * (cell[4] - kinetic)
    sound = jnp.sqrt(gamma_ratio * pressure * inverse)
    return velocity, pressure, sound


def side(cell, axis_num):
    velocity, pressure, sound = primitives(cell)
    along = velocity[axis_num]
    flux = [cell[1 + axis_num]]
    for d in range(3):
        term = cell[1 + d] * along
        flux.append(term + pressure if d == axis_num else term)
    flux.append((cell[4] + pressure) * along)
    return flux, jnp.abs(along) + sound


def axis_change(cell, speed, below, above, axis_num):
    flux_below, speed_below = side(below, axis_num)
    flux_above, speed_above = side(above, axis_num)
    speed_below = jnp.maximum(speed, speed_below)
    speed_above = jnp.maximum(speed, speed_above)
    return [
        0.5 * (flux_above[v] - flux_below[v])
        - 0.5 * (speed_above * (above[v] - cell[v]) - speed_below * (cell[v] - below[v]))
        for v in range(5)
    ]


def pack_kernel(slot_hbm, near_hbm, state_hbm, out_ref, pick_ref, slot_ref, near_ref, state_ref, sems):
    copies = [
        pltpu.make_async_copy(source, target, sems.at[i])
        for i, (source, target) in enumerate(
            (
                (state_hbm.at[0], state_ref.at[0]),
                (state_hbm.at[1], state_ref.at[1]),
                (slot_hbm, slot_ref),
                (near_hbm, near_ref),
            )
        )
    ]
    for copy in copies:
        copy.start()
    count = out_ref.shape[0] // SLOT
    boxes = 2 * count
    best = None
    for box in range(2):
        copies[box].wait()
        cell = [state_ref[box, v] for v in range(5)]
        for v in range(5):
            for half in range(2):
                row = ROWS * box + 2 * v + half
                out_ref[pl.ds(row, count, stride=SLOT), :] = cell[v][:, LANES * half : LANES * (half + 1)]
        velocity, _, sound = primitives(cell)
        largest = jnp.maximum(jnp.maximum(jnp.abs(velocity[0]), jnp.abs(velocity[1])), jnp.abs(velocity[2]))
        speed = largest + sound
        best = speed if best is None else jnp.maximum(best, speed)
    best = jnp.max(jnp.max(best, axis=0, keepdims=True), axis=1, keepdims=True)

    def place(index):
        local = lax.rem(index, boxes)
        return lax.rem(local, 2) * count + lax.div(local, 2)

    copies[2].wait()
    copies[3].wait()
    values = [place(slot_ref[0]), place(slot_ref[1])]
    for box in range(2):
        values += [place(near_ref[box, 2]), place(near_ref[box, 3])]
    lane = lane_index((count, LANES))
    header = jnp.where(lane == 6, jnp.broadcast_to(best, lane.shape), 0.0)
    for position, value in enumerate(values):
        header = jnp.where(lane == position, value.astype(jnp.float32), header)
    out_ref[pl.ds(20, count, stride=SLOT), :] = header
    for row in range(21, SLOT):
        out_ref[pl.ds(row, count, stride=SLOT), :] = jnp.zeros((count, LANES), jnp.float32)

    segment = lax.axis_index(SEG)
    lane = lane_index(pick_ref.shape)
    picks = jnp.zeros(pick_ref.shape, jnp.float32)
    for box in range(2):
        for face in (0, 1, 4, 5):
            index = near_ref[box, face]
            value = lax.rem(index, 2)
            if face < 2:
                value = value + jnp.where(lax.div(index, boxes) == segment, 2, 0)
            picks = jnp.where(lane == 6 * box + face, value.astype(jnp.float32), picks)
    pick_ref[...] = picks


def three_parts(value):
    high = value.astype(jnp.bfloat16)
    rest = value - high.astype(jnp.float32)
    middle = rest.astype(jnp.bfloat16)
    low = (rest - middle.astype(jnp.float32)).astype(jnp.bfloat16)
    return jnp.concatenate([high, middle, low], axis=0)


def gather_rows(one_hot, parts):
    chosen = jnp.where(one_hot, 1.0, 0.0).astype(jnp.bfloat16)
    return jnp.dot(jnp.concatenate([chosen] * 3, axis=1), parts, preferred_element_type=jnp.float32)


def route_kernel(in_ref, out_ref, best_ref):
    count = in_ref.shape[0] // SLOT
    boxes = 2 * count
    header = in_ref[pl.ds(20, count, stride=SLOT), :]
    best = jnp.max(jnp.where(lane_index(header.shape) == 6, header, 0.0), axis=0, keepdims=True)
    best = jnp.max(best, axis=1, keepdims=True)
    best_ref[...] = jnp.broadcast_to(best.reshape(1, 1, 1), best_ref.shape)
    both = jnp.concatenate([header, pltpu.roll(header, LANES - 1, 1)], axis=0)
    target = jnp.broadcast_to(jnp.transpose(both)[0:1, :], (boxes, boxes))
    index = lax.broadcasted_iota(jnp.int32, (boxes, boxes), 0).astype(jnp.float32)

    def beside(first, second):
        rows = jnp.concatenate([header[:, first : first + 1], header[:, second : second + 1]], axis=0)
        return jnp.broadcast_to(rows, (boxes, boxes))

    columns = []
    for row in range(ROWS):
        columns.append(
            jnp.concatenate(
                [in_ref[pl.ds(ROWS * box + row, count, stride=SLOT), :] for box in range(2)], axis=0
            )
        )
    lane2 = lane_index((boxes, LANES))
    last = jnp.zeros((boxes, LANES), jnp.float32)
    first = jnp.zeros((boxes, LANES), jnp.float32)
    for v in range(5):
        mine = (lane2 >= 16 * v) & (lane2 < 16 * (v + 1))
        last = jnp.where(mine, pltpu.roll(columns[2 * v + 1], 16 * (v + 1), 1), last)
        first = jnp.where(mine, pltpu.roll(columns[2 * v], 16 * v, 1) if v else columns[0], first)
    placed = gather_rows(index == target, three_parts(jnp.concatenate(columns, axis=1)))
    below = gather_rows(beside(2, 4) == target, three_parts(last))
    above = gather_rows(beside(3, 5) == target, three_parts(first))
    for box in range(2):
        rows = slice(count * box, count * (box + 1))
        for row in range(ROWS):
            out_ref[pl.ds(ROWS * box + row, count, stride=SLOT), :] = placed[rows, LANES * row : LANES * (row + 1)]
        out_ref[pl.ds(20 + box, count, stride=SLOT), :] = below[rows]
        out_ref[pl.ds(22 + box, count, stride=SLOT), :] = above[rows]


def change_kernel(pick_ref, in_ref, before_ref, after_ref, out_ref):
    count = in_ref.shape[0] // SLOT

    def rows_of(row):
        return in_ref[pl.ds(row, count, stride=SLOT), :]

    def pick(box, face):
        return pick_ref[0:1, 6 * box + face : 6 * box + face + 1]

    cell = [
        jnp.stack([rows_of(ROWS * box + 2 * v + half) for box in range(2) for half in range(2)]) for v in range(5)
    ]
    velocity, _, sound = primitives(cell)
    lane = lane_index(cell[0].shape)

    own = (in_ref[SLOT * (count - 1) : SLOT * count, :], in_ref[0:SLOT, :])
    other = (before_ref[...], after_ref[...])
    ghosts = []
    for face in range(2):
        for box in range(2):
            wanted = pick(box, face)
            rows = jnp.where(wanted >= 2.0, own[face], other[face])
            first = (wanted == 0.0) | (wanted == 2.0)
            ghosts.append(jnp.where(first, rows[0:ROWS], rows[ROWS : 2 * ROWS]))
    layer = lax.broadcasted_iota(jnp.int32, cell[0].shape, 1)
    below, above = [], []
    for v in range(5):

        def spread(rows):
            return jnp.stack([rows[box][2 * v + half : 2 * v + half + 1] for box in range(2) for half in range(2)])

        below.append(jnp.where(layer == 0, spread(ghosts[0:2]), pltpu.roll(cell[v], 1, 1)))
        above.append(jnp.where(layer == count - 1, spread(ghosts[2:4]), pltpu.roll(cell[v], count - 1, 1)))
    change = axis_change(cell, jnp.abs(velocity[0]) + sound, below, above, 0)

    ghost_low = [rows_of(20 + box) for box in range(2)]
    ghost_high = [rows_of(22 + box) for box in range(2)]
    below, above = [], []
    for v in range(5):
        low = [pltpu.roll(g, LANES - 16 * v, 1) if v else g for g in ghost_low]
        high = [pltpu.roll(g, 112 - 16 * v, 1) for g in ghost_high]
        rolled = pltpu.roll(cell[v], 16, 2)
        edge = jnp.stack([low[0], rolled[0], low[1], rolled[2]])
        below.append(jnp.where(lane < 16, edge, rolled))
        rolled = pltpu.roll(cell[v], LANES - 16, 2)
        edge = jnp.stack([rolled[1], high[0], rolled[3], high[1]])
        above.append(jnp.where(lane >= LANES - 16, edge, rolled))
    more = axis_change(cell, jnp.abs(velocity[1]) + sound, below, above, 1)
    change = [change[v] + more[v] for v in range(5)]

    deep = lane & 15
    below, above = [], []
    slots = [[pick(box, face) == 0.0 for box in range(2)] for face in (4, 5)]
    for v in range(5):
        wrapped = pltpu.roll(cell[v], LANES - 15, 2)
        edge = jnp.concatenate([jnp.where(slots[0][box], wrapped[0:2], wrapped[2:4]) for box in range(2)], axis=0)
        below.append(jnp.where(deep == 0, edge, pltpu.roll(cell[v], 1, 2)))
        wrapped = pltpu.roll(cell[v], 15, 2)
        edge = jnp.concatenate([jnp.where(slots[1][box], wrapped[0:2], wrapped[2:4]) for box in range(2)], axis=0)
        above.append(jnp.where(deep == 15, edge, pltpu.roll(cell[v], LANES - 1, 2)))
    more = axis_change(cell, jnp.abs(velocity[2]) + sound, below, above, 2)

    for v in range(5):
        out_ref[v] = change[v] + more[v]


def finish_kernel(in_ref, change_ref, best_ref, out_ref):
    count = in_ref.shape[0] // SLOT
    step = courant / jnp.max(best_ref[...], axis=0)
    for box in range(2):
        for v in range(5):
            for half in range(2):
                cell = in_ref[pl.ds(ROWS * box + 2 * v + half, count, stride=SLOT), :]
                columns = slice(LANES * half, LANES * (half + 1))
                out_ref[box, v, :, columns] = cell - step * change_ref[v, 2 * box + half]


def local(state, new_slot, neighbours):
    count = lax.axis_size("curve")
    along_x, along_z = (lax.axis_size(axis) for axis in SEG)
    segs = along_x * along_z
    f32 = jnp.float32
    sent, pick = pl.pallas_call(
        pack_kernel,
        out_shape=(jax.ShapeDtypeStruct((SLOT * count, LANES), f32), jax.ShapeDtypeStruct((8, LANES), f32)),
        in_specs=[hbm, hbm, hbm],
        out_specs=(vmem, vmem),
        scratch_shapes=[
            pltpu.SMEM(new_slot.shape, jnp.int32),
            pltpu.SMEM(neighbours.shape, jnp.int32),
            pltpu.VMEM(state.shape, f32),
            pltpu.SemaphoreType.DMA((4,)),
        ],
        name="pack",
    )(new_slot, neighbours, state)
    met = lax.all_to_all(sent.reshape(count, SLOT, LANES), "curve", 0, 0, tiled=True)
    routed, best = pl.pallas_call(
        route_kernel,
        out_shape=(
            jax.ShapeDtypeStruct((SLOT * count, LANES), f32),
            jax.ShapeDtypeStruct((along_z, 1, LANES), f32),
        ),
        in_specs=[vmem],
        out_specs=(vmem, vmem),
        compiler_params=params,
        name="route",
    )(met.reshape(SLOT * count, LANES))
    moved = lax.all_to_all(routed.reshape(count, SLOT, LANES), "curve", 0, 0, tiled=True)
    up = [(i, (i + 1) % segs) for i in range(segs)]
    down = [(j, i) for i, j in up]
    best = lax.all_to_all(best, SEG[1], 0, 0, tiled=True)
    before = lax.ppermute(moved[count - 1], SEG, up)
    after = lax.ppermute(moved[0], SEG, down)
    best = lax.all_gather(best, SEG[0], axis=0, tiled=True)
    moved = moved.reshape(SLOT * count, LANES)
    change = pl.pallas_call(
        change_kernel,
        out_shape=jax.ShapeDtypeStruct((5, 4, count, LANES), f32),
        in_specs=[vmem] * 4,
        out_specs=vmem,
        compiler_params=params,
        name="change",
    )(pick, moved, before, after)
    return pl.pallas_call(
        finish_kernel,
        out_shape=jax.ShapeDtypeStruct(state.shape, f32),
        in_specs=[vmem] * 3,
        out_specs=vmem,
        compiler_params=params,
        name="finish",
    )(moved, change, best)


def solution(mesh):
    segs, count = mesh.devices.shape
    side_x = math.isqrt(segs)
    grid = Mesh(mesh.devices.reshape(side_x, segs // side_x, count), SEG + ("curve",))
    placed = P(SEG + ("curve",))
    return jax.shard_map(
        local, mesh=grid, in_specs=(placed, placed, placed), out_specs=placed, check_vma=False
    )
```

```python
import math

import jax
import jax.numpy as jnp
from jax import lax
from jax.experimental import pallas as pl
from jax.experimental.pallas import tpu as pltpu
from jax.sharding import Mesh, PartitionSpec as P

gamma_ratio = 1.4
courant = 0.3

LANES = 128
SEG = ("seg_x", "seg_z")
ROWS = 10
SLOT = 24

vmem = pl.BlockSpec(memory_space=pltpu.VMEM)
hbm = pl.BlockSpec(memory_space=pltpu.HBM)
params = pltpu.CompilerParams(vmem_limit_bytes=16 * 2**20)


def lane_index(shape):
    return lax.broadcasted_iota(jnp.int32, shape, len(shape) - 1)


def primitives(cell):
    inverse = 1.0 / cell[0]
    velocity = [cell[1 + d] * inverse for d in range(3)]
    kinetic = 0.5 * (cell[1] * velocity[0] + cell[2] * velocity[1] + cell[3] * velocity[2])
    pressure = (gamma_ratio - 1.0) * (cell[4] - kinetic)
    sound = jnp.sqrt(gamma_ratio * pressure * inverse)
    return velocity, pressure, sound


def side(cell, axis_num):
    velocity, pressure, sound = primitives(cell)
    along = velocity[axis_num]
    flux = [cell[1 + axis_num]]
    for d in range(3):
        term = cell[1 + d] * along
        flux.append(term + pressure if d == axis_num else term)
    flux.append((cell[4] + pressure) * along)
    return flux, jnp.abs(along) + sound


def axis_change(cell, speed, below, above, axis_num):
    flux_below, speed_below = side(below, axis_num)
    flux_above, speed_above = side(above, axis_num)
    speed_below = jnp.maximum(speed, speed_below)
    speed_above = jnp.maximum(speed, speed_above)
    return [
        0.5 * (flux_above[v] - flux_below[v])
        - 0.5 * (speed_above * (above[v] - cell[v]) - speed_below * (cell[v] - below[v]))
        for v in range(5)
    ]


def pack_kernel(slot_hbm, near_hbm, state_hbm, out_ref, pick_ref, slot_ref, near_ref, state_ref, sems):
    copies = [
        pltpu.make_async_copy(source, target, sems.at[i])
        for i, (source, target) in enumerate(
            (
                (state_hbm.at[0], state_ref.at[0]),
                (state_hbm.at[1], state_ref.at[1]),
                (slot_hbm, slot_ref),
                (near_hbm, near_ref),
            )
        )
    ]
    for copy in copies:
        copy.start()
    count = out_ref.shape[0] // SLOT
    boxes = 2 * count
    best = None
    for box in range(2):
        copies[box].wait()
        cell = [state_ref[box, v] for v in range(5)]
        for v in range(5):
            for half in range(2):
                row = ROWS * box + 2 * v + half
                out_ref[pl.ds(row, count, stride=SLOT), :] = cell[v][:, LANES * half : LANES * (half + 1)]
        velocity, _, sound = primitives(cell)
        largest = jnp.maximum(jnp.maximum(jnp.abs(velocity[0]), jnp.abs(velocity[1])), jnp.abs(velocity[2]))
        speed = largest + sound
        best = speed if best is None else jnp.maximum(best, speed)
    best = jnp.max(jnp.max(best, axis=0, keepdims=True), axis=1, keepdims=True)

    def place(index):
        local = lax.rem(index, boxes)
        return lax.rem(local, 2) * count + lax.div(local, 2)

    copies[2].wait()
    copies[3].wait()
    values = [place(slot_ref[0]), place(slot_ref[1])]
    for box in range(2):
        values += [place(near_ref[box, 2]), place(near_ref[box, 3])]
    lane = lane_index((count, LANES))
    header = jnp.where(lane == 6, jnp.broadcast_to(best, lane.shape), 0.0)
    for position, value in enumerate(values):
        header = jnp.where(lane == position, value.astype(jnp.float32), header)
    out_ref[pl.ds(20, count, stride=SLOT), :] = header
    for row in range(21, SLOT):
        out_ref[pl.ds(row, count, stride=SLOT), :] = jnp.zeros((count, LANES), jnp.float32)

    segment = lax.axis_index(SEG)
    lane = lane_index(pick_ref.shape)
    picks = jnp.zeros(pick_ref.shape, jnp.float32)
    for box in range(2):
        for face in (0, 1, 4, 5):
            index = near_ref[box, face]
            value = lax.rem(index, 2)
            if face < 2:
                value = value + jnp.where(lax.div(index, boxes) == segment, 2, 0)
            picks = jnp.where(lane == 6 * box + face, value.astype(jnp.float32), picks)
    pick_ref[...] = picks


def three_parts(value):
    high = value.astype(jnp.bfloat16)
    rest = value - high.astype(jnp.float32)
    middle = rest.astype(jnp.bfloat16)
    low = (rest - middle.astype(jnp.float32)).astype(jnp.bfloat16)
    return jnp.concatenate([high, middle, low], axis=0)


def gather_rows(one_hot, parts):
    chosen = jnp.where(one_hot, 1.0, 0.0).astype(jnp.bfloat16)
    return jnp.dot(jnp.concatenate([chosen] * 3, axis=1), parts, preferred_element_type=jnp.float32)


def route_kernel(in_ref, out_ref, best_hbm, best_ref, sem):
    count = in_ref.shape[0] // SLOT
    boxes = 2 * count
    header = in_ref[pl.ds(20, count, stride=SLOT), :]
    best = jnp.max(jnp.where(lane_index(header.shape) == 6, header, 0.0), axis=0, keepdims=True)
    best = jnp.max(best, axis=1, keepdims=True)
    best_ref[...] = jnp.broadcast_to(best.reshape(1, 1, 1), best_ref.shape)
    copy = pltpu.make_async_copy(best_ref, best_hbm, sem)
    copy.start()
    both = jnp.concatenate([header, pltpu.roll(header, LANES - 1, 1)], axis=0)
    target = jnp.broadcast_to(jnp.transpose(both)[0:1, :], (boxes, boxes))
    index = lax.broadcasted_iota(jnp.int32, (boxes, boxes), 0).astype(jnp.float32)

    def beside(first, second):
        rows = jnp.concatenate([header[:, first : first + 1], header[:, second : second + 1]], axis=0)
        return jnp.broadcast_to(rows, (boxes, boxes))

    columns = []
    for row in range(ROWS):
        columns.append(
            jnp.concatenate(
                [in_ref[pl.ds(ROWS * box + row, count, stride=SLOT), :] for box in range(2)], axis=0
            )
        )
    lane2 = lane_index((boxes, LANES))
    last = jnp.zeros((boxes, LANES), jnp.float32)
    first = jnp.zeros((boxes, LANES), jnp.float32)
    for v in range(5):
        mine = (lane2 >= 16 * v) & (lane2 < 16 * (v + 1))
        last = jnp.where(mine, pltpu.roll(columns[2 * v + 1], 16 * (v + 1), 1), last)
        first = jnp.where(mine, pltpu.roll(columns[2 * v], 16 * v, 1) if v else columns[0], first)
    placed = gather_rows(index == target, three_parts(jnp.concatenate(columns, axis=1)))
    below = gather_rows(beside(2, 4) == target, three_parts(last))
    above = gather_rows(beside(3, 5) == target, three_parts(first))
    for box in range(2):
        rows = slice(count * box, count * (box + 1))
        for row in range(ROWS):
            out_ref[pl.ds(ROWS * box + row, count, stride=SLOT), :] = placed[rows, LANES * row : LANES * (row + 1)]
        out_ref[pl.ds(20 + box, count, stride=SLOT), :] = below[rows]
        out_ref[pl.ds(22 + box, count, stride=SLOT), :] = above[rows]
    copy.wait()


def peak_kernel(in_ref, out_ref):
    best = jnp.max(in_ref[...], axis=0, keepdims=True)
    out_ref[...] = jnp.broadcast_to(best, out_ref.shape)


def change_kernel(pick_ref, in_ref, before_ref, after_ref, out_ref):
    count = in_ref.shape[0] // SLOT

    def rows_of(row):
        return in_ref[pl.ds(row, count, stride=SLOT), :]

    def pick(box, face):
        return pick_ref[0:1, 6 * box + face : 6 * box + face + 1]

    cell = [
        jnp.stack([rows_of(ROWS * box + 2 * v + half) for box in range(2) for half in range(2)]) for v in range(5)
    ]
    velocity, _, sound = primitives(cell)
    lane = lane_index(cell[0].shape)

    own = (in_ref[SLOT * (count - 1) : SLOT * count, :], in_ref[0:SLOT, :])
    other = (before_ref[...], after_ref[...])
    ghosts = []
    for face in range(2):
        for box in range(2):
            wanted = pick(box, face)
            rows = jnp.where(wanted >= 2.0, own[face], other[face])
            first = (wanted == 0.0) | (wanted == 2.0)
            ghosts.append(jnp.where(first, rows[0:ROWS], rows[ROWS : 2 * ROWS]))
    layer = lax.broadcasted_iota(jnp.int32, cell[0].shape, 1)
    below, above = [], []
    for v in range(5):

        def spread(rows):
            return jnp.stack([rows[box][2 * v + half : 2 * v + half + 1] for box in range(2) for half in range(2)])

        below.append(jnp.where(layer == 0, spread(ghosts[0:2]), pltpu.roll(cell[v], 1, 1)))
        above.append(jnp.where(layer == count - 1, spread(ghosts[2:4]), pltpu.roll(cell[v], count - 1, 1)))
    change = axis_change(cell, jnp.abs(velocity[0]) + sound, below, above, 0)

    ghost_low = [rows_of(20 + box) for box in range(2)]
    ghost_high = [rows_of(22 + box) for box in range(2)]
    below, above = [], []
    for v in range(5):
        low = [pltpu.roll(g, LANES - 16 * v, 1) if v else g for g in ghost_low]
        high = [pltpu.roll(g, 112 - 16 * v, 1) for g in ghost_high]
        rolled = pltpu.roll(cell[v], 16, 2)
        edge = jnp.stack([low[0], rolled[0], low[1], rolled[2]])
        below.append(jnp.where(lane < 16, edge, rolled))
        rolled = pltpu.roll(cell[v], LANES - 16, 2)
        edge = jnp.stack([rolled[1], high[0], rolled[3], high[1]])
        above.append(jnp.where(lane >= LANES - 16, edge, rolled))
    more = axis_change(cell, jnp.abs(velocity[1]) + sound, below, above, 1)
    change = [change[v] + more[v] for v in range(5)]

    deep = lane & 15
    below, above = [], []
    slots = [[pick(box, face) == 0.0 for box in range(2)] for face in (4, 5)]
    for v in range(5):
        wrapped = pltpu.roll(cell[v], LANES - 15, 2)
        edge = jnp.concatenate([jnp.where(slots[0][box], wrapped[0:2], wrapped[2:4]) for box in range(2)], axis=0)
        below.append(jnp.where(deep == 0, edge, pltpu.roll(cell[v], 1, 2)))
        wrapped = pltpu.roll(cell[v], 15, 2)
        edge = jnp.concatenate([jnp.where(slots[1][box], wrapped[0:2], wrapped[2:4]) for box in range(2)], axis=0)
        above.append(jnp.where(deep == 15, edge, pltpu.roll(cell[v], LANES - 1, 2)))
    more = axis_change(cell, jnp.abs(velocity[2]) + sound, below, above, 2)

    for v in range(5):
        out_ref[v] = change[v] + more[v]


def finish_kernel(in_ref, change_ref, best_ref, out_hbm, out_ref, sems):
    count = in_ref.shape[0] // SLOT
    step = courant / jnp.max(best_ref[...], axis=0)
    for box in range(2):
        for v in range(5):
            for half in range(2):
                cell = in_ref[pl.ds(ROWS * box + 2 * v + half, count, stride=SLOT), :]
                columns = slice(LANES * half, LANES * (half + 1))
                out_ref[box, v, :, columns] = cell - step * change_ref[v, 2 * box + half]
        pltpu.make_async_copy(out_ref.at[box], out_hbm.at[box], sems.at[box]).start()
    for box in range(2):
        pltpu.make_async_copy(out_ref.at[box], out_hbm.at[box], sems.at[box]).wait()


def local(state, new_slot, neighbours):
    count = lax.axis_size("curve")
    along_x, along_z = (lax.axis_size(axis) for axis in SEG)
    segs = along_x * along_z
    f32 = jnp.float32
    sent, pick = pl.pallas_call(
        pack_kernel,
        out_shape=(jax.ShapeDtypeStruct((SLOT * count, LANES), f32), jax.ShapeDtypeStruct((8, LANES), f32)),
        in_specs=[hbm, hbm, hbm],
        out_specs=(vmem, vmem),
        scratch_shapes=[
            pltpu.SMEM(new_slot.shape, jnp.int32),
            pltpu.SMEM(neighbours.shape, jnp.int32),
            pltpu.VMEM(state.shape, f32),
            pltpu.SemaphoreType.DMA((4,)),
        ],
        name="pack",
    )(new_slot, neighbours, state)
    met = lax.all_to_all(sent.reshape(count, SLOT, LANES), "curve", 0, 0, tiled=True)
    routed, best = pl.pallas_call(
        route_kernel,
        out_shape=(
            jax.ShapeDtypeStruct((SLOT * count, LANES), f32),
            jax.ShapeDtypeStruct((along_z, 1, LANES), f32),
        ),
        in_specs=[vmem],
        out_specs=(vmem, hbm),
        scratch_shapes=[pltpu.VMEM((along_z, 1, LANES), f32), pltpu.SemaphoreType.DMA],
        compiler_params=params,
        name="route",
    )(met.reshape(SLOT * count, LANES))
    moved = lax.all_to_all(routed.reshape(count, SLOT, LANES), "curve", 0, 0, tiled=True)
    up = [(i, (i + 1) % segs) for i in range(segs)]
    down = [(j, i) for i, j in up]
    best = lax.all_to_all(best, SEG[1], 0, 0, tiled=True)
    before = lax.ppermute(moved[count - 1], SEG, up)
    after = lax.ppermute(moved[0], SEG, down)
    best = pl.pallas_call(
        peak_kernel,
        out_shape=jax.ShapeDtypeStruct((along_x, 1, LANES), f32),
        in_specs=[vmem],
        out_specs=vmem,
        compiler_params=params,
        name="peak",
    )(best)
    best = lax.all_to_all(best, SEG[0], 0, 0, tiled=True)
    moved = moved.reshape(SLOT * count, LANES)
    change = pl.pallas_call(
        change_kernel,
        out_shape=jax.ShapeDtypeStruct((5, 4, count, LANES), f32),
        in_specs=[vmem] * 4,
        out_specs=vmem,
        compiler_params=params,
        name="change",
    )(pick, moved, before, after)
    return pl.pallas_call(
        finish_kernel,
        out_shape=jax.ShapeDtypeStruct(state.shape, f32),
        in_specs=[vmem] * 3,
        out_specs=hbm,
        scratch_shapes=[pltpu.VMEM(state.shape, f32), pltpu.SemaphoreType.DMA((2,))],
        compiler_params=params,
        name="finish",
    )(moved, change, best)


def solution(mesh):
    segs, count = mesh.devices.shape
    side_x = math.isqrt(segs)
    grid = Mesh(mesh.devices.reshape(side_x, segs // side_x, count), SEG + ("curve",))
    placed = P(SEG + ("curve",))
    return jax.shard_map(
        local, mesh=grid, in_specs=(placed, placed, placed), out_specs=placed, check_vma=False
    )
```

```python
import math

import jax
import jax.numpy as jnp
from jax import lax
from jax.experimental import pallas as pl
from jax.experimental.pallas import tpu as pltpu
from jax.sharding import Mesh, PartitionSpec as P

gamma_ratio = 1.4
courant = 0.3

LANES = 128
SEG = ("seg_x", "seg_z")
ROWS = 10
SLOT = 24

vmem = pl.BlockSpec(memory_space=pltpu.VMEM)
hbm = pl.BlockSpec(memory_space=pltpu.HBM)
params = pltpu.CompilerParams(vmem_limit_bytes=16 * 2**20)


def lane_index(shape):
    return lax.broadcasted_iota(jnp.int32, shape, len(shape) - 1)


def primitives(cell):
    inverse = 1.0 / cell[0]
    velocity = [cell[1 + d] * inverse for d in range(3)]
    kinetic = 0.5 * (cell[1] * velocity[0] + cell[2] * velocity[1] + cell[3] * velocity[2])
    pressure = (gamma_ratio - 1.0) * (cell[4] - kinetic)
    sound = jnp.sqrt(gamma_ratio * pressure * inverse)
    return velocity, pressure, sound


def side(cell, axis_num):
    velocity, pressure, sound = primitives(cell)
    along = velocity[axis_num]
    flux = [cell[1 + axis_num]]
    for d in range(3):
        term = cell[1 + d] * along
        flux.append(term + pressure if d == axis_num else term)
    flux.append((cell[4] + pressure) * along)
    return flux, jnp.abs(along) + sound


def axis_change(cell, speed, below, above, axis_num):
    flux_below, speed_below = side(below, axis_num)
    flux_above, speed_above = side(above, axis_num)
    speed_below = jnp.maximum(speed, speed_below)
    speed_above = jnp.maximum(speed, speed_above)
    return [
        0.5 * (flux_above[v] - flux_below[v])
        - 0.5 * (speed_above * (above[v] - cell[v]) - speed_below * (cell[v] - below[v]))
        for v in range(5)
    ]


def pack_kernel(slot_hbm, near_hbm, state_hbm, out_ref, pick_ref, slot_ref, near_ref, state_ref, sems):
    copies = [
        pltpu.make_async_copy(source, target, sems.at[i])
        for i, (source, target) in enumerate(
            (
                (state_hbm.at[0], state_ref.at[0]),
                (state_hbm.at[1], state_ref.at[1]),
                (slot_hbm, slot_ref),
                (near_hbm, near_ref),
            )
        )
    ]
    for copy in copies:
        copy.start()
    count = out_ref.shape[0] // SLOT
    boxes = 2 * count
    best = None
    for box in range(2):
        copies[box].wait()
        cell = [state_ref[box, v] for v in range(5)]
        for v in range(5):
            for half in range(2):
                row = ROWS * box + 2 * v + half
                out_ref[pl.ds(row, count, stride=SLOT), :] = cell[v][:, LANES * half : LANES * (half + 1)]
        velocity, _, sound = primitives(cell)
        largest = jnp.maximum(jnp.maximum(jnp.abs(velocity[0]), jnp.abs(velocity[1])), jnp.abs(velocity[2]))
        speed = largest + sound
        best = speed if best is None else jnp.maximum(best, speed)
    best = jnp.max(jnp.max(best, axis=0, keepdims=True), axis=1, keepdims=True)

    def place(index):
        local = lax.rem(index, boxes)
        return lax.rem(local, 2) * count + lax.div(local, 2)

    copies[2].wait()
    copies[3].wait()
    values = [place(slot_ref[0]), place(slot_ref[1])]
    for box in range(2):
        values += [place(near_ref[box, 2]), place(near_ref[box, 3])]
    lane = lane_index((count, LANES))
    header = jnp.where(lane == 6, jnp.broadcast_to(best, lane.shape), 0.0)
    for position, value in enumerate(values):
        header = jnp.where(lane == position, value.astype(jnp.float32), header)
    out_ref[pl.ds(20, count, stride=SLOT), :] = header
    for row in range(21, SLOT):
        out_ref[pl.ds(row, count, stride=SLOT), :] = jnp.zeros((count, LANES), jnp.float32)

    segment = lax.axis_index(SEG)
    lane = lane_index(pick_ref.shape)
    picks = jnp.zeros(pick_ref.shape, jnp.float32)
    for box in range(2):
        for face in (0, 1, 4, 5):
            index = near_ref[box, face]
            value = lax.rem(index, 2)
            if face < 2:
                value = value + jnp.where(lax.div(index, boxes) == segment, 2, 0)
            picks = jnp.where(lane == 6 * box + face, value.astype(jnp.float32), picks)
    pick_ref[...] = picks


def three_parts(value):
    high = value.astype(jnp.bfloat16)
    rest = value - high.astype(jnp.float32)
    middle = rest.astype(jnp.bfloat16)
    low = (rest - middle.astype(jnp.float32)).astype(jnp.bfloat16)
    return jnp.concatenate([high, middle, low], axis=0)


def gather_rows(one_hot, parts):
    chosen = jnp.where(one_hot, 1.0, 0.0).astype(jnp.bfloat16)
    return jnp.dot(jnp.concatenate([chosen] * 3, axis=1), parts, preferred_element_type=jnp.float32)


def route_kernel(in_ref, out_ref, best_ref):
    count = in_ref.shape[0] // SLOT
    boxes = 2 * count
    header = in_ref[pl.ds(20, count, stride=SLOT), :]
    best = jnp.max(jnp.where(lane_index(header.shape) == 6, header, 0.0), axis=0, keepdims=True)
    best = jnp.max(best, axis=1, keepdims=True)
    best_ref[...] = jnp.broadcast_to(best.reshape(1, 1, 1), best_ref.shape)
    both = jnp.concatenate([header, pltpu.roll(header, LANES - 1, 1)], axis=0)
    target = jnp.broadcast_to(jnp.transpose(both)[0:1, :], (boxes, boxes))
    index = lax.broadcasted_iota(jnp.int32, (boxes, boxes), 0).astype(jnp.float32)

    def beside(first, second):
        rows = jnp.concatenate([header[:, first : first + 1], header[:, second : second + 1]], axis=0)
        return jnp.broadcast_to(rows, (boxes, boxes))

    columns = []
    for row in range(ROWS):
        columns.append(
            jnp.concatenate(
                [in_ref[pl.ds(ROWS * box + row, count, stride=SLOT), :] for box in range(2)], axis=0
            )
        )
    lane2 = lane_index((boxes, LANES))
    last = jnp.zeros((boxes, LANES), jnp.float32)
    first = jnp.zeros((boxes, LANES), jnp.float32)
    for v in range(5):
        mine = (lane2 >= 16 * v) & (lane2 < 16 * (v + 1))
        last = jnp.where(mine, pltpu.roll(columns[2 * v + 1], 16 * (v + 1), 1), last)
        first = jnp.where(mine, pltpu.roll(columns[2 * v], 16 * v, 1) if v else columns[0], first)
    placed = gather_rows(index == target, three_parts(jnp.concatenate(columns, axis=1)))
    below = gather_rows(beside(2, 4) == target, three_parts(last))
    above = gather_rows(beside(3, 5) == target, three_parts(first))
    for box in range(2):
        rows = slice(count * box, count * (box + 1))
        for row in range(ROWS):
            out_ref[pl.ds(ROWS * box + row, count, stride=SLOT), :] = placed[rows, LANES * row : LANES * (row + 1)]
        out_ref[pl.ds(20 + box, count, stride=SLOT), :] = below[rows]
        out_ref[pl.ds(22 + box, count, stride=SLOT), :] = above[rows]


def peak_kernel(in_ref, out_ref):
    best = jnp.max(in_ref[...], axis=0, keepdims=True)
    out_ref[...] = jnp.broadcast_to(best, out_ref.shape)


def change_kernel(pick_ref, in_ref, before_ref, after_ref, out_ref):
    count = in_ref.shape[0] // SLOT

    def rows_of(row):
        return in_ref[pl.ds(row, count, stride=SLOT), :]

    def pick(box, face):
        return pick_ref[0:1, 6 * box + face : 6 * box + face + 1]

    cell = [
        jnp.stack([rows_of(ROWS * box + 2 * v + half) for box in range(2) for half in range(2)]) for v in range(5)
    ]
    velocity, _, sound = primitives(cell)
    lane = lane_index(cell[0].shape)

    own = (in_ref[SLOT * (count - 1) : SLOT * count, :], in_ref[0:SLOT, :])
    other = (before_ref[...], after_ref[...])
    ghosts = []
    for face in range(2):
        for box in range(2):
            wanted = pick(box, face)
            rows = jnp.where(wanted >= 2.0, own[face], other[face])
            first = (wanted == 0.0) | (wanted == 2.0)
            ghosts.append(jnp.where(first, rows[0:ROWS], rows[ROWS : 2 * ROWS]))
    layer = lax.broadcasted_iota(jnp.int32, cell[0].shape, 1)
    below, above = [], []
    for v in range(5):

        def spread(rows):
            return jnp.stack([rows[box][2 * v + half : 2 * v + half + 1] for box in range(2) for half in range(2)])

        below.append(jnp.where(layer == 0, spread(ghosts[0:2]), pltpu.roll(cell[v], 1, 1)))
        above.append(jnp.where(layer == count - 1, spread(ghosts[2:4]), pltpu.roll(cell[v], count - 1, 1)))
    change = axis_change(cell, jnp.abs(velocity[0]) + sound, below, above, 0)

    ghost_low = [rows_of(20 + box) for box in range(2)]
    ghost_high = [rows_of(22 + box) for box in range(2)]
    below, above = [], []
    for v in range(5):
        low = [pltpu.roll(g, LANES - 16 * v, 1) if v else g for g in ghost_low]
        high = [pltpu.roll(g, 112 - 16 * v, 1) for g in ghost_high]
        rolled = pltpu.roll(cell[v], 16, 2)
        edge = jnp.stack([low[0], rolled[0], low[1], rolled[2]])
        below.append(jnp.where(lane < 16, edge, rolled))
        rolled = pltpu.roll(cell[v], LANES - 16, 2)
        edge = jnp.stack([rolled[1], high[0], rolled[3], high[1]])
        above.append(jnp.where(lane >= LANES - 16, edge, rolled))
    more = axis_change(cell, jnp.abs(velocity[1]) + sound, below, above, 1)
    change = [change[v] + more[v] for v in range(5)]

    deep = lane & 15
    below, above = [], []
    slots = [[pick(box, face) == 0.0 for box in range(2)] for face in (4, 5)]
    for v in range(5):
        wrapped = pltpu.roll(cell[v], LANES - 15, 2)
        edge = jnp.concatenate([jnp.where(slots[0][box], wrapped[0:2], wrapped[2:4]) for box in range(2)], axis=0)
        below.append(jnp.where(deep == 0, edge, pltpu.roll(cell[v], 1, 2)))
        wrapped = pltpu.roll(cell[v], 15, 2)
        edge = jnp.concatenate([jnp.where(slots[1][box], wrapped[0:2], wrapped[2:4]) for box in range(2)], axis=0)
        above.append(jnp.where(deep == 15, edge, pltpu.roll(cell[v], LANES - 1, 2)))
    more = axis_change(cell, jnp.abs(velocity[2]) + sound, below, above, 2)

    for v in range(5):
        out_ref[v] = change[v] + more[v]


def finish_kernel(in_ref, change_ref, best_ref, out_ref):
    count = in_ref.shape[0] // SLOT
    step = courant / jnp.max(best_ref[...], axis=0)
    for box in range(2):
        for v in range(5):
            for half in range(2):
                cell = in_ref[pl.ds(ROWS * box + 2 * v + half, count, stride=SLOT), :]
                columns = slice(LANES * half, LANES * (half + 1))
                out_ref[box, v, :, columns] = cell - step * change_ref[v, 2 * box + half]


def local(state, new_slot, neighbours):
    count = lax.axis_size("curve")
    along_x, along_z = (lax.axis_size(axis) for axis in SEG)
    segs = along_x * along_z
    f32 = jnp.float32
    sent, pick = pl.pallas_call(
        pack_kernel,
        out_shape=(jax.ShapeDtypeStruct((SLOT * count, LANES), f32), jax.ShapeDtypeStruct((8, LANES), f32)),
        in_specs=[hbm, hbm, hbm],
        out_specs=(vmem, vmem),
        scratch_shapes=[
            pltpu.SMEM(new_slot.shape, jnp.int32),
            pltpu.SMEM(neighbours.shape, jnp.int32),
            pltpu.VMEM(state.shape, f32),
            pltpu.SemaphoreType.DMA((4,)),
        ],
        name="pack",
    )(new_slot, neighbours, state)
    met = lax.all_to_all(sent.reshape(count, SLOT, LANES), "curve", 0, 0, tiled=True)
    routed, best = pl.pallas_call(
        route_kernel,
        out_shape=(
            jax.ShapeDtypeStruct((SLOT * count, LANES), f32),
            jax.ShapeDtypeStruct((along_z, 1, LANES), f32),
        ),
        in_specs=[vmem],
        out_specs=(vmem, vmem),
        compiler_params=params,
        name="route",
    )(met.reshape(SLOT * count, LANES))
    moved = lax.all_to_all(routed.reshape(count, SLOT, LANES), "curve", 0, 0, tiled=True)
    up = [(i, (i + 1) % segs) for i in range(segs)]
    down = [(j, i) for i, j in up]
    moved, best = lax.optimization_barrier((moved, best))
    best = lax.all_to_all(best, SEG[1], 0, 0, tiled=True)
    before = lax.ppermute(moved[count - 1], SEG, up)
    best = pl.pallas_call(
        peak_kernel,
        out_shape=jax.ShapeDtypeStruct((along_x, 1, LANES), f32),
        in_specs=[vmem],
        out_specs=vmem,
        compiler_params=params,
        name="peak",
    )(best)
    best, first = lax.optimization_barrier((best, moved[0]))
    after = lax.ppermute(first, SEG, down)
    best = lax.all_to_all(best, SEG[0], 0, 0, tiled=True)
    moved = moved.reshape(SLOT * count, LANES)
    change = pl.pallas_call(
        change_kernel,
        out_shape=jax.ShapeDtypeStruct((5, 4, count, LANES), f32),
        in_specs=[vmem] * 4,
        out_specs=vmem,
        compiler_params=params,
        name="change",
    )(pick, moved, before, after)
    return pl.pallas_call(
        finish_kernel,
        out_shape=jax.ShapeDtypeStruct(state.shape, f32),
        in_specs=[vmem] * 3,
        out_specs=vmem,
        compiler_params=params,
        name="finish",
    )(moved, change, best)


def solution(mesh):
    segs, count = mesh.devices.shape
    side_x = math.isqrt(segs)
    grid = Mesh(mesh.devices.reshape(side_x, segs // side_x, count), SEG + ("curve",))
    placed = P(SEG + ("curve",))
    return jax.shard_map(
        local, mesh=grid, in_specs=(placed, placed, placed), out_specs=placed, check_vma=False
    )
```

```python
import math

import jax
import jax.numpy as jnp
from jax import lax
from jax.experimental import pallas as pl
from jax.experimental.pallas import tpu as pltpu
from jax.sharding import Mesh, PartitionSpec as P

gamma_ratio = 1.4
courant = 0.3

LANES = 128
SEG = ("seg_x", "seg_z")
ROWS = 10
SLOT = 24

vmem = pl.BlockSpec(memory_space=pltpu.VMEM)
hbm = pl.BlockSpec(memory_space=pltpu.HBM)
params = pltpu.CompilerParams(vmem_limit_bytes=16 * 2**20)


def lane_index(shape):
    return lax.broadcasted_iota(jnp.int32, shape, len(shape) - 1)


def primitives(cell):
    inverse = 1.0 / cell[0]
    velocity = [cell[1 + d] * inverse for d in range(3)]
    kinetic = 0.5 * (cell[1] * velocity[0] + cell[2] * velocity[1] + cell[3] * velocity[2])
    pressure = (gamma_ratio - 1.0) * (cell[4] - kinetic)
    sound = jnp.sqrt(gamma_ratio * pressure * inverse)
    return velocity, pressure, sound


def side(cell, axis_num):
    velocity, pressure, sound = primitives(cell)
    along = velocity[axis_num]
    flux = [cell[1 + axis_num]]
    for d in range(3):
        term = cell[1 + d] * along
        flux.append(term + pressure if d == axis_num else term)
    flux.append((cell[4] + pressure) * along)
    return flux, jnp.abs(along) + sound


def axis_change(cell, speed, below, above, axis_num):
    flux_below, speed_below = side(below, axis_num)
    flux_above, speed_above = side(above, axis_num)
    speed_below = jnp.maximum(speed, speed_below)
    speed_above = jnp.maximum(speed, speed_above)
    return [
        0.5 * (flux_above[v] - flux_below[v])
        - 0.5 * (speed_above * (above[v] - cell[v]) - speed_below * (cell[v] - below[v]))
        for v in range(5)
    ]


def pack_kernel(slot_hbm, near_hbm, state_hbm, out_ref, pick_ref, slot_ref, near_ref, state_ref, sems):
    copies = [
        pltpu.make_async_copy(source, target, sems.at[i])
        for i, (source, target) in enumerate(
            (
                (state_hbm.at[0], state_ref.at[0]),
                (state_hbm.at[1], state_ref.at[1]),
                (slot_hbm, slot_ref),
                (near_hbm, near_ref),
            )
        )
    ]
    for copy in copies:
        copy.start()
    count = out_ref.shape[0] // SLOT
    boxes = 2 * count
    best = None
    for box in range(2):
        copies[box].wait()
        cell = [state_ref[box, v] for v in range(5)]
        for v in range(5):
            for half in range(2):
                row = ROWS * box + 2 * v + half
                out_ref[pl.ds(row, count, stride=SLOT), :] = cell[v][:, LANES * half : LANES * (half + 1)]
        velocity, _, sound = primitives(cell)
        largest = jnp.maximum(jnp.maximum(jnp.abs(velocity[0]), jnp.abs(velocity[1])), jnp.abs(velocity[2]))
        speed = largest + sound
        best = speed if best is None else jnp.maximum(best, speed)
    best = jnp.max(jnp.max(best, axis=0, keepdims=True), axis=1, keepdims=True)

    def place(index):
        local = lax.rem(index, boxes)
        return lax.rem(local, 2) * count + lax.div(local, 2)

    copies[2].wait()
    copies[3].wait()
    values = [place(slot_ref[0]), place(slot_ref[1])]
    for box in range(2):
        values += [place(near_ref[box, 2]), place(near_ref[box, 3])]
    lane = lane_index((count, LANES))
    header = jnp.where(lane == 6, jnp.broadcast_to(best, lane.shape), 0.0)
    for position, value in enumerate(values):
        header = jnp.where(lane == position, value.astype(jnp.float32), header)
    out_ref[pl.ds(20, count, stride=SLOT), :] = header
    for row in range(21, SLOT):
        out_ref[pl.ds(row, count, stride=SLOT), :] = jnp.zeros((count, LANES), jnp.float32)

    segment = lax.axis_index(SEG)
    lane = lane_index(pick_ref.shape)
    picks = jnp.zeros(pick_ref.shape, jnp.float32)
    for box in range(2):
        for face in (0, 1, 4, 5):
            index = near_ref[box, face]
            value = lax.rem(index, 2)
            if face < 2:
                value = value + jnp.where(lax.div(index, boxes) == segment, 2, 0)
            picks = jnp.where(lane == 6 * box + face, value.astype(jnp.float32), picks)
    pick_ref[...] = picks


def three_parts(value):
    high = value.astype(jnp.bfloat16)
    rest = value - high.astype(jnp.float32)
    middle = rest.astype(jnp.bfloat16)
    low = (rest - middle.astype(jnp.float32)).astype(jnp.bfloat16)
    return jnp.concatenate([high, middle, low], axis=0)


def gather_rows(one_hot, parts):
    chosen = jnp.where(one_hot, 1.0, 0.0).astype(jnp.bfloat16)
    return jnp.dot(jnp.concatenate([chosen] * 3, axis=1), parts, preferred_element_type=jnp.float32)


def route_kernel(in_ref, out_ref, best_ref):
    count = in_ref.shape[0] // SLOT
    boxes = 2 * count
    header = in_ref[pl.ds(20, count, stride=SLOT), :]
    best = jnp.max(jnp.where(lane_index(header.shape) == 6, header, 0.0), axis=0, keepdims=True)
    best = jnp.max(best, axis=1, keepdims=True)
    best_ref[...] = jnp.broadcast_to(best.reshape(1, 1, 1), best_ref.shape)
    both = jnp.concatenate([header, pltpu.roll(header, LANES - 1, 1)], axis=0)
    target = jnp.broadcast_to(jnp.transpose(both)[0:1, :], (boxes, boxes))
    index = lax.broadcasted_iota(jnp.int32, (boxes, boxes), 0).astype(jnp.float32)

    def beside(first, second):
        rows = jnp.concatenate([header[:, first : first + 1], header[:, second : second + 1]], axis=0)
        return jnp.broadcast_to(rows, (boxes, boxes))

    columns = []
    for row in range(ROWS):
        columns.append(
            jnp.concatenate(
                [in_ref[pl.ds(ROWS * box + row, count, stride=SLOT), :] for box in range(2)], axis=0
            )
        )
    lane2 = lane_index((boxes, LANES))
    last = jnp.zeros((boxes, LANES), jnp.float32)
    first = jnp.zeros((boxes, LANES), jnp.float32)
    for v in range(5):
        mine = (lane2 >= 16 * v) & (lane2 < 16 * (v + 1))
        last = jnp.where(mine, pltpu.roll(columns[2 * v + 1], 16 * (v + 1), 1), last)
        first = jnp.where(mine, pltpu.roll(columns[2 * v], 16 * v, 1) if v else columns[0], first)
    placed = gather_rows(index == target, three_parts(jnp.concatenate(columns, axis=1)))
    below = gather_rows(beside(2, 4) == target, three_parts(last))
    above = gather_rows(beside(3, 5) == target, three_parts(first))
    for box in range(2):
        rows = slice(count * box, count * (box + 1))
        for row in range(ROWS):
            out_ref[pl.ds(ROWS * box + row, count, stride=SLOT), :] = placed[rows, LANES * row : LANES * (row + 1)]
        out_ref[pl.ds(20 + box, count, stride=SLOT), :] = below[rows]
        out_ref[pl.ds(22 + box, count, stride=SLOT), :] = above[rows]


def peak_kernel(in_ref, out_ref):
    best = jnp.max(in_ref[...], axis=0, keepdims=True)
    out_ref[...] = jnp.broadcast_to(best, out_ref.shape)


def change_kernel(pick_ref, in_ref, after_ref, before_ref, out_ref):
    count = in_ref.shape[0] // SLOT

    def rows_of(row):
        return in_ref[pl.ds(row, count, stride=SLOT), :]

    def pick(box, face):
        return pick_ref[0:1, 6 * box + face : 6 * box + face + 1]

    cell = [
        jnp.stack([rows_of(ROWS * box + 2 * v + half) for box in range(2) for half in range(2)]) for v in range(5)
    ]
    velocity, _, sound = primitives(cell)
    lane = lane_index(cell[0].shape)

    own = (in_ref[SLOT * (count - 1) : SLOT * count, :], in_ref[0:SLOT, :])
    other = (before_ref[...], after_ref[...])
    ghosts = []
    for face in range(2):
        for box in range(2):
            wanted = pick(box, face)
            rows = jnp.where(wanted >= 2.0, own[face], other[face])
            first = (wanted == 0.0) | (wanted == 2.0)
            ghosts.append(jnp.where(first, rows[0:ROWS], rows[ROWS : 2 * ROWS]))
    layer = lax.broadcasted_iota(jnp.int32, cell[0].shape, 1)
    below, above = [], []
    for v in range(5):

        def spread(rows):
            return jnp.stack([rows[box][2 * v + half : 2 * v + half + 1] for box in range(2) for half in range(2)])

        below.append(jnp.where(layer == 0, spread(ghosts[0:2]), pltpu.roll(cell[v], 1, 1)))
        above.append(jnp.where(layer == count - 1, spread(ghosts[2:4]), pltpu.roll(cell[v], count - 1, 1)))
    change = axis_change(cell, jnp.abs(velocity[0]) + sound, below, above, 0)

    ghost_low = [rows_of(20 + box) for box in range(2)]
    ghost_high = [rows_of(22 + box) for box in range(2)]
    below, above = [], []
    for v in range(5):
        low = [pltpu.roll(g, LANES - 16 * v, 1) if v else g for g in ghost_low]
        high = [pltpu.roll(g, 112 - 16 * v, 1) for g in ghost_high]
        rolled = pltpu.roll(cell[v], 16, 2)
        edge = jnp.stack([low[0], rolled[0], low[1], rolled[2]])
        below.append(jnp.where(lane < 16, edge, rolled))
        rolled = pltpu.roll(cell[v], LANES - 16, 2)
        edge = jnp.stack([rolled[1], high[0], rolled[3], high[1]])
        above.append(jnp.where(lane >= LANES - 16, edge, rolled))
    more = axis_change(cell, jnp.abs(velocity[1]) + sound, below, above, 1)
    change = [change[v] + more[v] for v in range(5)]

    deep = lane & 15
    below, above = [], []
    slots = [[pick(box, face) == 0.0 for box in range(2)] for face in (4, 5)]
    for v in range(5):
        wrapped = pltpu.roll(cell[v], LANES - 15, 2)
        edge = jnp.concatenate([jnp.where(slots[0][box], wrapped[0:2], wrapped[2:4]) for box in range(2)], axis=0)
        below.append(jnp.where(deep == 0, edge, pltpu.roll(cell[v], 1, 2)))
        wrapped = pltpu.roll(cell[v], 15, 2)
        edge = jnp.concatenate([jnp.where(slots[1][box], wrapped[0:2], wrapped[2:4]) for box in range(2)], axis=0)
        above.append(jnp.where(deep == 15, edge, pltpu.roll(cell[v], LANES - 1, 2)))
    more = axis_change(cell, jnp.abs(velocity[2]) + sound, below, above, 2)

    for v in range(5):
        out_ref[v] = change[v] + more[v]


def finish_kernel(in_ref, change_ref, best_ref, out_ref):
    count = in_ref.shape[0] // SLOT
    step = courant / jnp.max(best_ref[...], axis=0)
    for box in range(2):
        for v in range(5):
            for half in range(2):
                cell = in_ref[pl.ds(ROWS * box + 2 * v + half, count, stride=SLOT), :]
                columns = slice(LANES * half, LANES * (half + 1))
                out_ref[box, v, :, columns] = cell - step * change_ref[v, 2 * box + half]


def local(state, new_slot, neighbours):
    count = lax.axis_size("curve")
    along_x, along_z = (lax.axis_size(axis) for axis in SEG)
    segs = along_x * along_z
    f32 = jnp.float32
    sent, pick = pl.pallas_call(
        pack_kernel,
        out_shape=(jax.ShapeDtypeStruct((SLOT * count, LANES), f32), jax.ShapeDtypeStruct((8, LANES), f32)),
        in_specs=[hbm, hbm, hbm],
        out_specs=(vmem, vmem),
        scratch_shapes=[
            pltpu.SMEM(new_slot.shape, jnp.int32),
            pltpu.SMEM(neighbours.shape, jnp.int32),
            pltpu.VMEM(state.shape, f32),
            pltpu.SemaphoreType.DMA((4,)),
        ],
        name="pack",
    )(new_slot, neighbours, state)
    met = lax.all_to_all(sent.reshape(count, SLOT, LANES), "curve", 0, 0, tiled=True)
    routed, best = pl.pallas_call(
        route_kernel,
        out_shape=(
            jax.ShapeDtypeStruct((SLOT * count, LANES), f32),
            jax.ShapeDtypeStruct((along_z, 1, LANES), f32),
        ),
        in_specs=[vmem],
        out_specs=(vmem, vmem),
        compiler_params=params,
        name="route",
    )(met.reshape(SLOT * count, LANES))
    moved = lax.all_to_all(routed.reshape(count, SLOT, LANES), "curve", 0, 0, tiled=True)
    up = [(i, (i + 1) % segs) for i in range(segs)]
    down = [(j, i) for i, j in up]
    best = lax.all_to_all(best, SEG[1], 0, 0, tiled=True)
    after = lax.ppermute(moved[0], SEG, down)
    before = lax.ppermute(moved[count - 1], SEG, up)
    best = pl.pallas_call(
        peak_kernel,
        out_shape=jax.ShapeDtypeStruct((along_x, 1, LANES), f32),
        in_specs=[vmem],
        out_specs=vmem,
        compiler_params=params,
        name="peak",
    )(best)
    best = lax.all_to_all(best, SEG[0], 0, 0, tiled=True)
    moved = moved.reshape(SLOT * count, LANES)
    change = pl.pallas_call(
        change_kernel,
        out_shape=jax.ShapeDtypeStruct((5, 4, count, LANES), f32),
        in_specs=[vmem] * 4,
        out_specs=vmem,
        compiler_params=params,
        name="change",
    )(pick, moved, after, before)
    return pl.pallas_call(
        finish_kernel,
        out_shape=jax.ShapeDtypeStruct(state.shape, f32),
        in_specs=[vmem] * 3,
        out_specs=vmem,
        compiler_params=params,
        name="finish",
    )(moved, change, best)


def solution(mesh):
    segs, count = mesh.devices.shape
    side_x = math.isqrt(segs)
    grid = Mesh(mesh.devices.reshape(side_x, segs // side_x, count), SEG + ("curve",))
    placed = P(SEG + ("curve",))
    return jax.shard_map(
        local, mesh=grid, in_specs=(placed, placed, placed), out_specs=placed, check_vma=False
    )
```
